512 devices in a mesh: point: 8 (over z_hi, core), space: 64 (over z_lo, x, y).
Axes of the slice: x: 4, y: 4, z: 16 (z_hi: 4, z_lo: 4; z = z_hi * 4 + z_lo), core: 2. Of those that a mesh axis runs over, the one named last changes fastest.
Arguments:
- adjoint: float32 [8, 4, 128, 256, 128], P('point', None, 'space'), may hold values from -6 to 6
- fwd_velocity: bfloat16 [8, 3, 128, 256, 128], P('point', None, 'space'), may hold values from -6 to 6
- reynolds: float32 [8], P('point'), may hold values from 100 to 2000
- weights: int32 [8], replicated, may hold values from 1 to 64
- porosity: float32 [128, 256, 128], P('space'), may hold values from 0.05 to 1
- flags: int32 [128, 256, 128], P('space'), may hold values from 0 to 2, as said below
Outputs:
- adjoint_out: float32 [8, 4, 128, 256, 128], P('point', None, 'space')
- porosity_new: float32 [128, 256, 128], P('space')
The draws below stay inside these ranges and needn't reach their ends.
Inputs may be any that keep to these rules, and one draw needn't show every extreme that they name: `flags`: 1 marks a box of 128 x 64 cells (128 along the second dimension, 64 along the third, at a position that varies by draw) on the first plane, 2 such a box on the last plane, 0 elsewhere.
All inputs are finite; a program needn't handle non-finite values. Where the reference program divides by a largest or mean magnitude, that divisor is 1e-20 or more.
Results may differ from the reference program's by a relative error of at most 0.0003.
Values sent between devices are 32-bit elements; how exact they have to be, the bound alone decides.
No kernel may reach another device: no remote copies, remote signals or barrier semaphores. Data moves between devices by JAX's collectives and lax.ppermute only.
A program may use at most 64 MiB of HBM per device.

```python
import math
import jax
import jax.numpy as jnp
from jax import lax

NY = 256
NZ = 128
SWEEPS = 2
POINTS = 8
NX = 128


def draw_flags(key, part):
    key = jax.random.fold_in(key, 11)
    keys = jax.random.split(key, 4)
    shape = (NX, NY, NZ)
    xpos = jax.lax.broadcasted_iota(jnp.int32, shape, 0)
    ypos = jax.lax.broadcasted_iota(jnp.int32, shape, 1)
    zpos = jax.lax.broadcasted_iota(jnp.int32, shape, 2)
    in_y0 = jax.random.randint(keys[0], (), 0, NY // 2 + 1)
    in_z0 = jax.random.randint(keys[1], (), 0, NZ // 2 + 1)
    out_y0 = jax.random.randint(keys[2], (), 0, NY // 2 + 1)
    out_z0 = jax.random.randint(keys[3], (), 0, NZ // 2 + 1)
    inlet = (xpos == 0) & (ypos >= in_y0) & (ypos < in_y0 + NY // 2) & (zpos >= in_z0) & (zpos < in_z0 + NZ // 2)
    outlet = (xpos == NX - 1) & (ypos >= out_y0) & (ypos < out_y0 + NY // 2) & (zpos >= out_z0) & (zpos < out_z0 + NZ // 2)
    return jnp.where(inlet, 1, jnp.where(outlet, 2, 0)).astype(jnp.int32)


def plant(result, key, least, largest):
    longest = result.shape.index(max(result.shape))
    spots = []
    for shift in (0, 1):
        where = [jax.random.randint(jax.random.fold_in(key, axis), (), 0, length) for axis, length in enumerate(result.shape)]
        where[longest] = (where[longest] + shift) % result.shape[longest]
        spots.append(tuple(where))
    return result.at[spots[0]].set(least).at[spots[1]].set(largest)


def levels(rng, shape, cuts, least, largest):
    def one(dim, shards_of):
        draws = jax.random.uniform(jax.random.fold_in(jax.random.fold_in(rng, 6), dim), (shards_of,), jnp.float32, least / len(cuts), largest / len(cuts))
        return jnp.repeat(jnp.exp(draws), shape[dim] // shards_of).reshape((-1,) + (1,) * (len(shape) - dim - 1))

    loudness = one(*cuts[0])
    for cut in cuts[1:]:
        loudness = loudness * one(*cut)
    return loudness


def scatter_about(own_key, extent, spread, limit, pieces=(), held_as=jnp.bfloat16):
    result = jax.random.normal(own_key, extent, jnp.float32) * spread
    if len(pieces) > 0:
        result = levels(own_key, extent, pieces, -0.22, 0.18) * result
    return jnp.clip(result, min=-limit, max=limit).astype(held_as)


def setup_inputs(seed: int = 0) -> dict:
    splits = jax.random.split(jax.random.key(seed), 7)
    return {
        "adjoint": scatter_about(splits[0], (POINTS, 4, NX, NY, NZ), 1.0, 6.0, ((0, 8), (2, 64)), jnp.float32),
        "fwd_velocity": scatter_about(splits[1], (POINTS, 3, NX, NY, NZ), 1.0, 6.0, ((0, 8), (2, 64))),
        "reynolds": jnp.clip(jnp.exp(math.log(2000.0) - 2.9957323 * jax.random.uniform(splits[2], (POINTS,), jnp.float32) ** levels(splits[2], (POINTS,), ((0, 8),), -0.2, 0.2)), 100.0, 2000.0),
        "weights": plant(jax.random.randint(splits[3], (POINTS,), 1, 65), jax.random.fold_in(splits[3], 1), 1, 64).astype(jnp.int32),
        "porosity": jnp.clip(0.05 + 0.95 * jax.random.uniform(splits[4], (NX, NY, NZ), jnp.float32) ** levels(splits[4], (NX, NY, NZ), ((0, 64),), -0.2, 0.2), 0.05, 1.0),
        "flags": draw_flags(jax.random.fold_in(splits[6], 71), 0),
    }


AMAX = 50.0
QRAMP = 0.1
BETA = 0.5
STEP = 0.2
EPS = 1e-6


def view(padded, dx, dy, dz):
    xs = padded.shape[-3] - 2
    ys = padded.shape[-2] - 2
    zs = padded.shape[-1] - 2
    return padded[..., 1 + dx:1 + dx + xs, 1 + dy:1 + dy + ys, 1 + dz:1 + dz + zs]


def sweep(state, velocity, alpha, open_cells, outlet, viscosity, padded):
    offsets = [(1, 0, 0), (0, 1, 0), (0, 0, 1)]
    plus = [view(padded, a, b, c) for (a, b, c) in offsets]
    minus = [view(padded, -a, -b, -c) for (a, b, c) in offsets]
    lam = state[:3]
    neighbours = plus[0][:3] + minus[0][:3] + plus[1][:3] + minus[1][:3] + plus[2][:3] + minus[2][:3]
    advect = 0.5 * (velocity[0] * (plus[0][:3] - minus[0][:3]) + velocity[1] * (plus[1][:3] - minus[1][:3]) + velocity[2] * (plus[2][:3] - minus[2][:3]))
    gradient = jnp.stack([0.5 * (plus[d][3] - minus[d][3]) for d in range(3)])
    diverge = 0.5 * ((plus[0][0] - minus[0][0]) + (plus[1][1] - minus[1][1]) + (plus[2][2] - minus[2][2]))
    source = velocity * (outlet - alpha)
    lam_new = open_cells * (lam + viscosity * neighbours + advect - gradient + source) / (1.0 + 6.0 * viscosity + alpha)
    mu_new = state[3] - BETA * diverge
    return jnp.concatenate([lam_new, mu_new[None]], axis=0)


def filter_sum(padded):
    total = jnp.zeros(view(padded, 0, 0, 0).shape, jnp.float32)
    for dx in (-1, 0, 1):
        for dy in (-1, 0, 1):
            for dz in (-1, 0, 1):
                weight = (2.0 - abs(dx)) * (2.0 - abs(dy)) * (2.0 - abs(dz))
                total = total + weight * view(padded, dx, dy, dz)
    return total


def reference(adjoint, fwd_velocity, reynolds, weights, porosity, flags):
    alpha = AMAX * QRAMP * (1.0 - porosity) / (QRAMP + porosity)
    dalpha = -AMAX * QRAMP * (1.0 + QRAMP) / ((QRAMP + porosity) ** 2)
    open_cells = (flags != 1).astype(jnp.float32)
    outlet = (flags == 2).astype(jnp.float32)
    viscosity = 20.0 / reynolds
    share = weights.astype(jnp.float32) / jnp.sum(weights.astype(jnp.float32))

    def one_point(items):
        state, velocity_bf, visc = items
        velocity = velocity_bf.astype(jnp.float32)
        for step in range(SWEEPS):
            padded = jnp.pad(state, ((0, 0), (1, 1), (1, 1), (1, 1)))
            state = sweep(state, velocity, alpha, open_cells, outlet, visc, padded)
        return state

    final = lax.map(one_point, (adjoint, fwd_velocity, viscosity))

    def accumulate(total, items):
        state, velocity_bf, weight = items
        velocity = velocity_bf.astype(jnp.float32)
        return total + weight * jnp.sum(velocity * state[:3], axis=0), None

    summed, unused = lax.scan(accumulate, jnp.zeros(porosity.shape, jnp.float32), (final, fwd_velocity, share))
    sens = dalpha * summed
    filtered = filter_sum(jnp.pad(sens, 1)) / filter_sum(jnp.pad(jnp.ones_like(sens), 1))
    gmax = jnp.max(jnp.abs(filtered))
    porosity_new = jnp.clip(porosity - STEP * filtered / (gmax + EPS), 0.0, 1.0)
    return final, porosity_new
```

```python
import functools

import jax
import jax.numpy as jnp
from jax import lax
from jax.experimental import pallas as pl
from jax.experimental.pallas import tpu as pltpu
from jax.sharding import Mesh
from jax.sharding import PartitionSpec as P

AMAX = 50.0
QRAMP = 0.1
BETA = 0.5
STEP = 0.2
EPS = 1e-06

POINT = ("zhi", "core")
SPACE = ("zlo", "x", "y")
CHUNK = 32
VM = pl.BlockSpec(memory_space=pltpu.VMEM)
SM = pl.BlockSpec(memory_space=pltpu.SMEM)
F32 = jnp.float32


def shape(*dims):
    return jax.ShapeDtypeStruct(dims, F32)


def call(body, ins, outs, scratch=(), flops=1_000_000, moved=4_000_000):
    return pl.pallas_call(
        body,
        in_specs=ins,
        out_specs=[VM] * len(outs),
        out_shape=list(outs),
        scratch_shapes=list(scratch),
        compiler_params=pltpu.CompilerParams(vmem_limit_bytes=32 * 1024 * 1024),
        cost_estimate=pl.CostEstimate(flops=flops, bytes_accessed=moved, transcendentals=0),
    )


def row_shift(read, r, size, rows):
    at = lax.broadcasted_iota(jnp.int32, (size, 128), 0)
    if r == 0:
        before = jnp.where(at == 0, 0.0, pltpu.roll(read(0, size), 1, 0))
    else:
        before = read(r - 1, size)
    if r + size == rows:
        after = jnp.where(at == size - 1, 0.0, pltpu.roll(read(r, size), size - 1, 0))
    else:
        after = read(r + 1, size)
    return before, after


def lane_shift(value):
    at = lax.broadcasted_iota(jnp.int32, value.shape, 1)
    last = value.shape[1] - 1
    before = jnp.where(at == 0, 0.0, pltpu.roll(value, 1, 1))
    after = jnp.where(at == last, 0.0, pltpu.roll(value, last, 1))
    return before, after


def local_chunk(read, p, r, size, rows, vel, nu, scale, drive):
    u = [vel[0, d, p, r : r + size].astype(F32) for d in range(3)]
    ux, uy, uz = [0.5 * v for v in u]
    inner = nu + ux if p == 0 else nu - ux
    outer = nu - ux if p == 0 else nu + ux
    y_after, y_before = nu + uy, nu - uy
    z_after, z_before = nu + uz, nu - uz
    sign = 1.0 if p == 0 else -1.0
    mu = read(3, p, r, size)
    mu_in = read(3, 1 - p, r, size)
    mu_ym, mu_yp = row_shift(lambda a, n: read(3, p, a, n), r, size, rows)
    mu_zm, mu_zp = lane_shift(mu)
    gradient = [(0.5 * sign) * mu_in, 0.5 * (mu_yp - mu_ym), 0.5 * (mu_zp - mu_zm)]
    parts = []
    diverge = None
    for c in range(3):
        lam = read(c, p, r, size)
        lam_in = read(c, 1 - p, r, size)
        ym, yp = row_shift(lambda a, n: read(c, p, a, n), r, size, rows)
        zm, zp = lane_shift(lam)
        total = lam + inner * lam_in + y_after * yp + y_before * ym + z_after * zp + z_before * zm
        total = total - gradient[c] + u[c] * drive
        parts.append(scale * total)
        term = (sign * lam_in, yp - ym, zp - zm)[c]
        diverge = term if diverge is None else diverge + term
    parts.append(mu - (0.5 * BETA) * diverge)
    return parts, scale * outer, u


def viscosity_of(reynolds):
    return 20.0 / jnp.full((1, 128), reynolds[0], F32)


def first_local(reynolds, adjoint, vel, porosity, flags, part, factor, scaled):
    rows = adjoint.shape[3]
    nu = viscosity_of(reynolds)
    read = lambda c, p, r, n: adjoint[0, c, p, r : r + n]
    for p in range(2):
        for r in range(0, rows, CHUNK):
            now = slice(r, r + CHUNK)
            por = porosity[p, now]
            flag = flags[p, now]
            alpha = (AMAX * QRAMP) * (1.0 - por) / (QRAMP + por)
            scale = jnp.where(flag != 1, 1.0, 0.0) / (1.0 + 6.0 * nu + alpha)
            drive = jnp.where(flag == 2, 1.0, 0.0) - alpha
            parts, outer, _ = local_chunk(read, p, r, CHUNK, rows, vel, nu, scale, drive)
            for c in range(4):
                part[c, p, now] = parts[c]
            factor[p, now] = outer
            scaled[p, now] = scale


def join(part, factor, scaled, halo, p, now):
    sign = 1.0 if p == 0 else -1.0
    held = [halo[c, now] for c in range(4)]
    outer = factor[p, now]
    lam = [part[c, p, now] + outer * held[c] for c in range(3)]
    lam[0] = lam[0] + (0.5 * sign) * (scaled[p, now] * held[3])
    mu = part[3, p, now] + (0.5 * BETA * sign) * held[0]
    return lam, mu


def first_join(part, factor, scaled, before, after, plane0, plane1):
    rows = before.shape[1]
    for p, halo, out in ((0, before, plane0), (1, after, plane1)):
        for r in range(0, rows, CHUNK):
            now = slice(r, r + CHUNK)
            lam, mu = join(part, factor, scaled, halo, p, now)
            for c in range(3):
                out[c, now] = lam[c]
            out[3, now] = mu


def second_local(reynolds, weights, where, plane0, plane1, vel, porosity, flags, scaled, part, pull):
    rows = plane0.shape[1]
    nu = viscosity_of(reynolds)
    whole = weights[0]
    for i in range(1, weights.shape[0]):
        whole = whole + weights[i]
    share = jnp.full((1, 128), weights[where[0]].astype(F32), F32) / jnp.full(
        (1, 128), whole.astype(F32), F32
    )
    planes = (plane0, plane1)
    read = lambda c, p, r, n: planes[p][c, r : r + n]
    for p in range(2):
        for r in range(0, rows, CHUNK):
            now = slice(r, r + CHUNK)
            por = porosity[p, now]
            inverse = 1.0 / (QRAMP + por)
            alpha = (AMAX * QRAMP) * (1.0 - por) * inverse
            drive = jnp.where(flags[p, now] == 2, 1.0, 0.0) - alpha
            parts, _, u = local_chunk(read, p, r, CHUNK, rows, vel, nu, scaled[p, now], drive)
            slope = (-AMAX * QRAMP * (1.0 + QRAMP)) * (inverse * inverse) * share
            for c in range(4):
                part[c, p, now] = parts[c]
            for c in range(3):
                pull[c, p, now] = slope * u[c]


def counts(at, whole):
    return 4.0 - jnp.where(at == 0, 1.0, 0.0) - jnp.where(at == whole - 1, 1.0, 0.0)


def second_join(where, part, factor, scaled, pull, before, after, state, mine, theirs, sens):
    rows = before.shape[1]
    for p, halo in ((0, before), (1, after)):
        for r in range(0, rows, CHUNK):
            now = slice(r, r + CHUNK)
            lam, mu = join(part, factor, scaled, halo, p, now)
            for c in range(3):
                state[0, c, p, now] = lam[c]
            state[0, 3, p, now] = mu
            sens[p, now] = pull[0, p, now] * lam[0] + pull[1, p, now] * lam[1] + pull[2, p, now] * lam[2]
    half = rows // 2
    core = where[1]
    lane = lax.broadcasted_iota(jnp.int32, (CHUNK, 128), 1)
    row = lax.broadcasted_iota(jnp.int32, (CHUNK, 128), 0)
    for p in range(2):
        for r in range(0, rows, CHUNK):
            read = lambda a, n: sens[p, a : a + n]
            ym, yp = row_shift(read, r, CHUNK, rows)
            along = ym + yp + 2.0 * read(r, CHUNK)
            zm, zp = lane_shift(along)
            total = (zm + zp + 2.0 * along) / (counts(row + r, rows) * counts(lane, 128))
            owner = r // half
            to = slice(r - owner * half, r - owner * half + CHUNK)

            @pl.when(core == owner)
            def _():
                mine[p, to] = total

            @pl.when(core != owner)
            def _():
                theirs[p, to] = total


def add_cores(mine, other, blocks):
    n, _, part, _ = blocks.shape
    for q in range(n):
        now = slice(q * part, (q + 1) * part)
        blocks[q] = mine[:, now] + other[:, now]


def add_points(blocks, low, high):
    total = blocks[0]
    for q in range(1, blocks.shape[0]):
        total = total + blocks[q]
    low[...] = total[0]
    high[...] = total[1]


def filter_rows(where, low, high, before, after, packed, spread):
    part = low.shape[0]
    x = where[2]
    whole = where[3]
    first = low[...]
    second = high[...]
    none = jnp.zeros((part, 128), jnp.int32)
    one = (before[...] + 2.0 * first + second) / counts(none + x, whole)
    two = (first + 2.0 * second + after[...]) / counts(none + (x + 1), whole)
    packed[0:part] = one
    packed[part : 2 * part] = two
    largest = jnp.max(jnp.maximum(jnp.abs(one), jnp.abs(two)))
    packed[2 * part :] = jnp.full((8, 128), largest, F32)
    spread[...] = jnp.full(spread.shape, largest, F32)


def with_largest(packed, found, out):
    rows = packed.shape[0] - 8
    largest = jnp.full((8, 128), jnp.max(found[...]), F32)
    for q in range(out.shape[0]):
        out[q, 0:rows] = packed[0:rows]
        out[q, rows:] = largest


def update(where, porosity, own, other, out):
    n = own.shape[0]
    part = (own.shape[1] - 8) // 2
    half = n * part
    largest = jnp.max(jnp.maximum(own[:, 2 * part :], other[:, 2 * part :]))
    factor = STEP / jnp.full((1, 128), largest + EPS, F32)
    core = where[1]
    for held, base in ((own, core * half), (other, half - core * half)):
        for p in range(2):
            for q in range(n):
                to = pl.ds(pl.multiple_of(base + q * part, part), part)
                moved = porosity[p, to] - factor * held[q, p * part : (p + 1) * part]
                out[p, to] = jnp.clip(moved, 0.0, 1.0)


def shards(adjoint, fwd_velocity, reynolds, weights, porosity, flags):
    planes, rows, depth = porosity.shape
    points = lax.axis_size("zhi")
    cores = lax.axis_size("core")
    spaces = lax.axis_size("zlo") * lax.axis_size("x") * lax.axis_size("y")
    part = rows // (points * cores)
    core = lax.axis_index("core")
    place = (lax.axis_index("zlo") * lax.axis_size("x") + lax.axis_index("x")) * lax.axis_size("y")
    place = place + lax.axis_index("y")
    where = jnp.stack(
        [
            lax.axis_index("zhi") * cores + core,
            core,
            place * planes,
            jnp.int32(planes * spaces),
        ]
    ).astype(jnp.int32)
    up = [(i, i + 1) for i in range(spaces - 1)]
    down = [(j, i) for i, j in up]

    def neighbours(low, high):
        return lax.ppermute(high, SPACE, up), lax.ppermute(low, SPACE, down)

    before, after = neighbours(adjoint[0, :, 0], adjoint[0, :, 1])
    half_state = shape(4, planes, rows, depth)
    field = shape(planes, rows, depth)
    plane = shape(4, rows, depth)
    part1, factor, scaled = call(first_local, [SM, VM, VM, VM, VM], [half_state, field, field])(
        reynolds, adjoint, fwd_velocity, porosity, flags
    )
    plane0, plane1 = call(first_join, [VM] * 5, [plane, plane])(
        part1, factor, scaled, before, after
    )
    before, after = neighbours(plane0, plane1)
    part2, pull = call(
        second_local,
        [SM, SM, SM] + [VM] * 6,
        [half_state, shape(3, planes, rows, depth)],
    )(reynolds, weights, where, plane0, plane1, fwd_velocity, porosity, flags, scaled)
    half = shape(planes, rows // cores, depth)
    state, mine, theirs = call(
        second_join,
        [SM] + [VM] * 6,
        [shape(1, 4, planes, rows, depth), half, half],
        scratch=[pltpu.VMEM((planes, rows, depth), F32)],
    )(where, part2, factor, scaled, pull, before, after)
    other = lax.ppermute(theirs, "core", [(0, 1), (1, 0)])
    (blocks,) = call(add_cores, [VM, VM], [shape(points, planes, part, depth)])(mine, other)
    blocks = lax.all_to_all(blocks, "zhi", 0, 0, tiled=True)
    low, high = call(add_points, [VM], [shape(part, depth)] * 2)(blocks)
    before, after = neighbours(low, high)
    packed, spread = call(
        filter_rows,
        [SM] + [VM] * 4,
        [shape(planes * part + 8, depth), shape(spaces, 1, depth)],
    )(where, low, high, before, after)
    found = lax.all_to_all(spread, SPACE, 0, 0, tiled=True)
    (copies,) = call(with_largest, [VM, VM], [shape(points, planes * part + 8, depth)])(
        packed, found
    )
    own = lax.all_to_all(copies, "zhi", 0, 0, tiled=True)
    other = lax.ppermute(own, "core", [(0, 1), (1, 0)])
    (porosity_new,) = call(update, [SM, VM, VM, VM], [field])(where, porosity, own, other)
    return state, porosity_new


def solution(mesh):
    fine = Mesh(mesh.devices.reshape(4, 2, 4, 4, 4), POINT + SPACE)
    return jax.shard_map(
        shards,
        mesh=fine,
        in_specs=(
            P(POINT, None, SPACE, None, None),
            P(POINT, None, SPACE, None, None),
            P(POINT),
            P(),
            P(SPACE, None, None),
            P(SPACE, None, None),
        ),
        out_specs=(P(POINT, None, SPACE, None, None), P(SPACE, None, None)),
        check_vma=False,
    )
```

```python
import functools

import jax
import jax.numpy as jnp
from jax import lax
from jax.experimental import pallas as pl
from jax.experimental.pallas import tpu as pltpu
from jax.sharding import Mesh
from jax.sharding import PartitionSpec as P

AMAX = 50.0
QRAMP = 0.1
BETA = 0.5
STEP = 0.2
EPS = 1e-06

POINT = ("zhi", "core")
SPACE = ("zlo", "x", "y")
CHUNK = 32
VM = pl.BlockSpec(memory_space=pltpu.VMEM)
SM = pl.BlockSpec(memory_space=pltpu.SMEM)
HB = pl.BlockSpec(memory_space=pltpu.HBM)
F32 = jnp.float32


def shape(*dims):
    return jax.ShapeDtypeStruct(dims, F32)


def call(body, ins, outs, specs=None, scratch=(), flops=1_000_000, moved=4_000_000):
    return pl.pallas_call(
        body,
        in_specs=ins,
        out_specs=[VM] * len(outs) if specs is None else specs,
        out_shape=list(outs),
        scratch_shapes=list(scratch),
        compiler_params=pltpu.CompilerParams(vmem_limit_bytes=32 * 1024 * 1024),
        cost_estimate=pl.CostEstimate(flops=flops, bytes_accessed=moved, transcendentals=0),
    )


def row_shift(read, r, size, rows):
    at = lax.broadcasted_iota(jnp.int32, (size, 128), 0)
    if r == 0:
        before = jnp.where(at == 0, 0.0, pltpu.roll(read(0, size), 1, 0))
    else:
        before = read(r - 1, size)
    if r + size == rows:
        after = jnp.where(at == size - 1, 0.0, pltpu.roll(read(r, size), size - 1, 0))
    else:
        after = read(r + 1, size)
    return before, after


def lane_shift(value):
    at = lax.broadcasted_iota(jnp.int32, value.shape, 1)
    last = value.shape[1] - 1
    before = jnp.where(at == 0, 0.0, pltpu.roll(value, 1, 1))
    after = jnp.where(at == last, 0.0, pltpu.roll(value, last, 1))
    return before, after


def side(where, p):
    odd = where[4]
    index = odd if p == 0 else 1 - odd
    return index, (1 - 2 * index).astype(F32)


def take_planes(where, adjoint, near, far, sems):
    copies = [
        pltpu.make_async_copy(adjoint.at[0, :, side(where, p)[0]], out, sems.at[p])
        for p, out in ((0, near), (1, far))
    ]
    for copy in copies:
        copy.start()
    for copy in copies:
        copy.wait()


def local_chunk(read, p, sign, r, size, rows, u, nu, scale, drive):
    ux, uy, uz = [0.5 * v for v in u]
    inner = nu + sign * ux
    outer = nu - sign * ux
    y_after, y_before = nu + uy, nu - uy
    z_after, z_before = nu + uz, nu - uz
    mu = read(3, p, r, size)
    mu_in = read(3, 1 - p, r, size)
    mu_ym, mu_yp = row_shift(lambda a, n: read(3, p, a, n), r, size, rows)
    mu_zm, mu_zp = lane_shift(mu)
    gradient = [(0.5 * sign) * mu_in, 0.5 * (mu_yp - mu_ym), 0.5 * (mu_zp - mu_zm)]
    parts = []
    diverge = None
    for c in range(3):
        lam = read(c, p, r, size)
        lam_in = read(c, 1 - p, r, size)
        ym, yp = row_shift(lambda a, n: read(c, p, a, n), r, size, rows)
        zm, zp = lane_shift(lam)
        total = lam + inner * lam_in + y_after * yp + y_before * ym + z_after * zp + z_before * zm
        total = total - gradient[c] + u[c] * drive
        parts.append(scale * total)
        term = (sign * lam_in, yp - ym, zp - zm)[c]
        diverge = term if diverge is None else diverge + term
    parts.append(mu - (0.5 * BETA) * diverge)
    return parts, scale * outer


def viscosity_of(reynolds):
    return 20.0 / jnp.full((1, 128), reynolds[0], F32)


def first_local(reynolds, where, near, far, vel, porosity, flags, part, factor, scaled):
    rows = near.shape[1]
    nu = viscosity_of(reynolds)
    planes = (near, far)
    read = lambda c, p, r, n: planes[p][c, r : r + n]
    for p in range(2):
        index, sign = side(where, p)
        for r in range(0, rows, CHUNK):
            now = slice(r, r + CHUNK)
            por = porosity[index, now]
            flag = flags[index, now]
            alpha = (AMAX * QRAMP) * (1.0 - por) / (QRAMP + por)
            scale = jnp.where(flag != 1, 1.0, 0.0) / (1.0 + 6.0 * nu + alpha)
            drive = jnp.where(flag == 2, 1.0, 0.0) - alpha
            u = [vel[0, d, index, now].astype(F32) for d in range(3)]
            parts, outer = local_chunk(read, p, sign, r, CHUNK, rows, u, nu, scale, drive)
            for c in range(4):
                part[c, p, now] = parts[c]
            factor[p, now] = outer
            scaled[p, now] = scale


def join(part, factor, scaled, halo, p, sign, now):
    held = [halo[c, now] for c in range(4)]
    outer = factor[p, now]
    lam = [part[c, p, now] + outer * held[c] for c in range(3)]
    lam[0] = lam[0] + (0.5 * sign) * (scaled[p, now] * held[3])
    mu = part[3, p, now] + (0.5 * BETA * sign) * held[0]
    return lam, mu


def first_join(p, where, part, factor, scaled, halo, out):
    _, sign = side(where, p)
    for r in range(0, halo.shape[1], CHUNK):
        now = slice(r, r + CHUNK)
        lam, mu = join(part, factor, scaled, halo, p, sign, now)
        for c in range(3):
            out[c, now] = lam[c]
        out[3, now] = mu


def second_local(reynolds, weights, where, near, far, vel, porosity, flags, scaled, part, pull):
    rows = near.shape[1]
    nu = viscosity_of(reynolds)
    whole = weights[0]
    for i in range(1, weights.shape[0]):
        whole = whole + weights[i]
    share = jnp.full((1, 128), weights[where[0]].astype(F32), F32) / jnp.full(
        (1, 128), whole.astype(F32), F32
    )
    planes = (near, far)
    read = lambda c, p, r, n: planes[p][c, r : r + n]
    for p in range(2):
        index, sign = side(where, p)
        for r in range(0, rows, CHUNK):
            now = slice(r, r + CHUNK)
            por = porosity[index, now]
            inverse = 1.0 / (QRAMP + por)
            alpha = (AMAX * QRAMP) * (1.0 - por) * inverse
            drive = jnp.where(flags[index, now] == 2, 1.0, 0.0) - alpha
            u = [vel[0, d, index, now].astype(F32) for d in range(3)]
            parts, _ = local_chunk(read, p, sign, r, CHUNK, rows, u, nu, scaled[p, now], drive)
            slope = (-AMAX * QRAMP * (1.0 + QRAMP)) * (inverse * inverse) * share
            for c in range(4):
                part[c, p, now] = parts[c]
            for c in range(3):
                pull[c, p, now] = slope * u[c]


def counts(at, whole):
    return 4.0 - jnp.where(at == 0, 1.0, 0.0) - jnp.where(at == whole - 1, 1.0, 0.0)


def second_join(where, part, factor, scaled, pull, near, far, state, mine, theirs, held, sens, sems):
    rows = near.shape[1]
    copies = []
    for p, halo in ((0, near), (1, far)):
        index, sign = side(where, p)
        for r in range(0, rows, CHUNK):
            now = slice(r, r + CHUNK)
            lam, mu = join(part, factor, scaled, halo, p, sign, now)
            for c in range(3):
                held[p, c, now] = lam[c]
            held[p, 3, now] = mu
            sens[p, now] = pull[0, p, now] * lam[0] + pull[1, p, now] * lam[1] + pull[2, p, now] * lam[2]
        copy = pltpu.make_async_copy(held.at[p], state.at[0, :, index], sems.at[p])
        copy.start()
        copies.append(copy)
    half = rows // 2
    core = where[1]
    lane = lax.broadcasted_iota(jnp.int32, (CHUNK, 128), 1)
    row = lax.broadcasted_iota(jnp.int32, (CHUNK, 128), 0)
    for p in range(2):
        index, _ = side(where, p)
        for r in range(0, rows, CHUNK):
            read = lambda a, n: sens[p, a : a + n]
            ym, yp = row_shift(read, r, CHUNK, rows)
            along = ym + yp + 2.0 * read(r, CHUNK)
            zm, zp = lane_shift(along)
            total = (zm + zp + 2.0 * along) / (counts(row + r, rows) * counts(lane, 128))
            owner = r // half
            to = slice(r - owner * half, r - owner * half + CHUNK)

            @pl.when(core == owner)
            def _():
                mine[index, to] = total

            @pl.when(core != owner)
            def _():
                theirs[index, to] = total

    for copy in copies:
        copy.wait()


def left_half(shape):
    return lax.broadcasted_iota(jnp.int32, shape, 1) < shape[1] // 2


def swap_halves(value):
    return pltpu.roll(value, value.shape[1] // 2, 1)


def interleave(one, two):
    left = left_half(one.shape)
    return jnp.where(left, one, swap_halves(two)), jnp.where(left, swap_halves(one), two)


def add_cores(mine, other, blocks):
    half = mine.shape[1]
    for r in range(0, half, CHUNK):
        now = slice(r, r + CHUNK)
        first, second = interleave(mine[0, now] + other[0, now], mine[1, now] + other[1, now])
        blocks[now] = first
        blocks[half + r : half + r + CHUNK] = second


def filter_planes(points, blocks, out):
    slabs = blocks.shape[0] // points
    total = blocks[0:slabs]
    for q in range(1, points):
        total = total + blocks[q * slabs : (q + 1) * slabs]
    swapped = swap_halves(total)
    at = lax.broadcasted_iota(jnp.int32, total.shape, 0)
    left = left_half(total.shape)
    below = jnp.where(at == 0, 0.0, pltpu.roll(swapped, 1, 0))
    above = jnp.where(at == slabs - 1, 0.0, pltpu.roll(swapped, slabs - 1, 0))
    plane = 2 * at + jnp.where(left, 0, 1)
    filtered = (2.0 * total + swapped + jnp.where(left, below, above)) / counts(plane, 2 * slabs)
    largest = jnp.full(total.shape, jnp.max(jnp.abs(filtered)), F32)
    for q in range(points):
        out[pl.ds(2 * q * slabs, slabs, stride=2)] = filtered
        out[pl.ds(2 * q * slabs + 1, slabs, stride=2)] = largest


def update(where, porosity, own, other, out):
    n = own.shape[0] // 2
    half = n // 2
    ends = [ref[pl.ds(1, n, stride=2)] for ref in (own, other)]
    largest = jnp.max(jnp.maximum(ends[0], ends[1]))
    factor = STEP / jnp.full((1, 128), largest + EPS, F32)
    core = where[1]
    for held, base in ((own, core * half), (other, half - core * half)):
        for r in range(0, half, CHUNK):
            to = pl.ds(pl.multiple_of(base + r, CHUNK), CHUNK)
            first = held[pl.ds(2 * r, CHUNK, stride=2)]
            second = held[pl.ds(2 * (half + r), CHUNK, stride=2)]
            for p, moved in enumerate(interleave(first, second)):
                out[p, to] = jnp.clip(porosity[p, to] - factor * moved, 0.0, 1.0)


def shards(adjoint, fwd_velocity, reynolds, weights, porosity, flags):
    planes, rows, depth = porosity.shape
    points = lax.axis_size("zhi")
    cores = lax.axis_size("core")
    spaces = lax.axis_size("zlo") * lax.axis_size("x") * lax.axis_size("y")
    core = lax.axis_index("core")
    place = (lax.axis_index("zlo") * lax.axis_size("x") + lax.axis_index("x")) * lax.axis_size("y")
    place = place + lax.axis_index("y")
    where = jnp.stack(
        [
            lax.axis_index("zhi") * cores + core,
            core,
            place * planes,
            jnp.int32(planes * spaces),
            place % 2,
        ]
    ).astype(jnp.int32)

    def pairs(start):
        there = [(i, i + 1) for i in range(start, spaces - 1, 2)]
        return there + [(j, i) for i, j in there]

    def swap(value, start):
        return lax.ppermute(value, SPACE, pairs(start))

    half_state = shape(4, planes, rows, depth)
    field = shape(planes, rows, depth)
    plane = shape(4, rows, depth)
    near, far = call(
        take_planes,
        [SM, HB],
        [plane, plane],
        scratch=[pltpu.SemaphoreType.DMA((2,))],
    )(where, adjoint)
    halo_near = swap(near, 1)
    halo_far = swap(far, 0)
    part, factor, scaled = call(first_local, [SM, SM] + [VM] * 5, [half_state, field, field])(
        reynolds, where, near, far, fwd_velocity, porosity, flags
    )
    ins = [SM] + [VM] * 4
    (near,) = call(functools.partial(first_join, 0), ins, [plane])(
        where, part, factor, scaled, halo_near
    )
    halo_near = swap(near, 1)
    (far,) = call(functools.partial(first_join, 1), ins, [plane])(
        where, part, factor, scaled, halo_far
    )
    halo_far = swap(far, 0)
    part, pull = call(
        second_local,
        [SM, SM, SM] + [VM] * 6,
        [half_state, shape(3, planes, rows, depth)],
    )(reynolds, weights, where, near, far, fwd_velocity, porosity, flags, scaled)
    half = shape(planes, rows // cores, depth)
    state, mine, theirs = call(
        second_join,
        [SM] + [VM] * 6,
        [shape(1, 4, planes, rows, depth), half, half],
        specs=[HB, VM, VM],
        scratch=[
            pltpu.VMEM((planes, 4, rows, depth), F32),
            pltpu.VMEM((planes, rows, depth), F32),
            pltpu.SemaphoreType.DMA((2,)),
        ],
    )(where, part, factor, scaled, pull, halo_near, halo_far)
    other = lax.ppermute(theirs, "core", [(0, 1), (1, 0)])
    group = points * spaces
    (blocks,) = call(add_cores, [VM, VM], [shape(group, depth)])(mine, other)
    blocks = lax.all_to_all(blocks.reshape(group, 1, depth), ("zhi",) + SPACE, 0, 0, tiled=True)
    (copies,) = call(functools.partial(filter_planes, points), [VM], [shape(2 * group, depth)])(
        blocks.reshape(group, depth)
    )
    own = lax.all_to_all(copies.reshape(group, 2, depth), ("zhi",) + SPACE, 0, 0, tiled=True)
    own = own.reshape(2 * group, depth)
    other = lax.ppermute(own, "core", [(0, 1), (1, 0)])
    (porosity_new,) = call(update, [SM, VM, VM, VM], [field])(where, porosity, own, other)
    return state, porosity_new


def solution(mesh):
    fine = Mesh(mesh.devices.reshape(4, 2, 4, 4, 4), POINT + SPACE)
    return jax.shard_map(
        shards,
        mesh=fine,
        in_specs=(
            P(POINT, None, SPACE, None, None),
            P(POINT, None, SPACE, None, None),
            P(POINT),
            P(),
            P(SPACE, None, None),
            P(SPACE, None, None),
        ),
        out_specs=(P(POINT, None, SPACE, None, None), P(SPACE, None, None)),
        check_vma=False,
    )
```

```python
import functools

import jax
import jax.numpy as jnp
from jax import lax
from jax.experimental import pallas as pl
from jax.experimental.pallas import tpu as pltpu
from jax.sharding import Mesh
from jax.sharding import PartitionSpec as P

AMAX = 50.0
QRAMP = 0.1
BETA = 0.5
STEP = 0.2
EPS = 1e-06

POINT = ("zhi", "core")
SPACE = ("zlo", "x", "y")
CHUNK = 32
VM = pl.BlockSpec(memory_space=pltpu.VMEM)
SM = pl.BlockSpec(memory_space=pltpu.SMEM)
HB = pl.BlockSpec(memory_space=pltpu.HBM)
F32 = jnp.float32


def shape(*dims):
    return jax.ShapeDtypeStruct(dims, F32)


def call(body, ins, outs, specs=None, scratch=(), vmem=32.0):
    return pl.pallas_call(
        body,
        in_specs=ins,
        out_specs=[VM] * len(outs) if specs is None else specs,
        out_shape=list(outs),
        scratch_shapes=list(scratch),
        compiler_params=pltpu.CompilerParams(vmem_limit_bytes=int(vmem * 2**20)),
        cost_estimate=pl.CostEstimate(flops=1_000_000, bytes_accessed=4_000_000, transcendentals=0),
    )


def row_shift(read, r, size, rows):
    at = lax.broadcasted_iota(jnp.int32, (size, 128), 0)
    if r == 0:
        before = jnp.where(at == 0, 0.0, pltpu.roll(read(0, size), 1, 0))
    else:
        before = read(r - 1, size)
    if r + size == rows:
        after = jnp.where(at == size - 1, 0.0, pltpu.roll(read(r, size), size - 1, 0))
    else:
        after = read(r + 1, size)
    return before, after


def lane_shift(value):
    at = lax.broadcasted_iota(jnp.int32, value.shape, 1)
    last = value.shape[1] - 1
    before = jnp.where(at == 0, 0.0, pltpu.roll(value, 1, 1))
    after = jnp.where(at == last, 0.0, pltpu.roll(value, last, 1))
    return before, after


def side(p):
    place = lax.axis_index("zlo") * lax.axis_size("x") + lax.axis_index("x")
    odd = lax.rem(place * lax.axis_size("y") + lax.axis_index("y"), 2)
    index = odd if p == 0 else 1 - odd
    return index, (1 - 2 * index).astype(F32)


def reader(first, second, far):
    def read(c, p, r, n):
        if p == 1:
            return far[c, r : r + n]
        if c in (1, 2):
            return second[c - 1, r : r + n]
        return first[min(c, 1), r : r + n]

    return read


def take_planes(adjoint, first, second, far):
    index, _ = side(0)
    for r in range(0, far.shape[1], CHUNK):
        now = slice(r, r + CHUNK)
        first[0, now] = adjoint[0, 0, index, now]
        first[1, now] = adjoint[0, 3, index, now]
        for c in range(2):
            second[c, now] = adjoint[0, c + 1, index, now]
        for c in range(4):
            far[c, now] = adjoint[0, c, 1 - index, now]


def local_chunk(read, p, sign, r, size, rows, u, nu, scale, drive):
    ux, uy, uz = [0.5 * v for v in u]
    inner = nu + sign * ux
    outer = nu - sign * ux
    y_after, y_before = nu + uy, nu - uy
    z_after, z_before = nu + uz, nu - uz
    mu = read(3, p, r, size)
    mu_in = read(3, 1 - p, r, size)
    mu_ym, mu_yp = row_shift(lambda a, n: read(3, p, a, n), r, size, rows)
    mu_zm, mu_zp = lane_shift(mu)
    gradient = [(0.5 * sign) * mu_in, 0.5 * (mu_yp - mu_ym), 0.5 * (mu_zp - mu_zm)]
    parts = []
    diverge = None
    for c in range(3):
        lam = read(c, p, r, size)
        lam_in = read(c, 1 - p, r, size)
        ym, yp = row_shift(lambda a, n: read(c, p, a, n), r, size, rows)
        zm, zp = lane_shift(lam)
        total = lam + inner * lam_in + y_after * yp + y_before * ym + z_after * zp + z_before * zm
        total = total - gradient[c] + u[c] * drive
        parts.append(scale * total)
        term = (sign * lam_in, yp - ym, zp - zm)[c]
        diverge = term if diverge is None else diverge + term
    parts.append(mu - (0.5 * BETA) * diverge)
    return parts, scale * outer


def viscosity_of(reynolds):
    return 20.0 / jnp.full((1, 128), reynolds[0], F32)


def first_local(reynolds, first, second, far, vel, porosity, flags, part, factor, scaled):
    rows = far.shape[1]
    nu = viscosity_of(reynolds)
    read = reader(first, second, far)
    for p in range(2):
        index, sign = side(p)
        for r in range(0, rows, CHUNK):
            now = slice(r, r + CHUNK)
            por = porosity[index, now]
            flag = flags[index, now]
            alpha = (AMAX * QRAMP) * (1.0 - por) / (QRAMP + por)
            scale = jnp.where(flag != 1, 1.0, 0.0) / (1.0 + 6.0 * nu + alpha)
            drive = jnp.where(flag == 2, 1.0, 0.0) - alpha
            u = [vel[0, d, index, now].astype(F32) for d in range(3)]
            parts, outer = local_chunk(read, p, sign, r, CHUNK, rows, u, nu, scale, drive)
            for c in range(4):
                part[c, p, now] = parts[c]
            factor[p, now] = outer
            scaled[p, now] = scale


def join_first(part, factor, scaled, halo, p, sign, now):
    lam, mu = halo
    outer = part[0, p, now] + factor[p, now] * lam + (0.5 * sign) * (scaled[p, now] * mu)
    return outer, part[3, p, now] + (0.5 * BETA * sign) * lam


def join_second(part, factor, halo, p, now):
    outer = factor[p, now]
    return [part[c + 1, p, now] + outer * halo[c] for c in range(2)]


def near_first(part, factor, scaled, halo, out):
    _, sign = side(0)
    for r in range(0, halo.shape[1], CHUNK):
        now = slice(r, r + CHUNK)
        out[0, now], out[1, now] = join_first(
            part, factor, scaled, (halo[0, now], halo[1, now]), 0, sign, now
        )


def near_second(part, factor, halo, after, out):
    for r in range(0, halo.shape[1], CHUNK):
        now = slice(r, r + CHUNK)
        out[0, now], out[1, now] = join_second(part, factor, (halo[0, now], halo[1, now]), 0, now)


def far_all(part, factor, scaled, halo, after, out):
    _, sign = side(1)
    for r in range(0, halo.shape[1], CHUNK):
        now = slice(r, r + CHUNK)
        out[0, now], out[3, now] = join_first(
            part, factor, scaled, (halo[0, now], halo[3, now]), 1, sign, now
        )
        out[1, now], out[2, now] = join_second(part, factor, (halo[1, now], halo[2, now]), 1, now)


def second_local(
    reynolds, weights, first, second, far, vel, porosity, flags, scaled, part, pull
):
    rows = far.shape[1]
    point = lax.axis_index("zhi") * lax.axis_size("core") + lax.axis_index("core")
    nu = viscosity_of(reynolds)
    whole = weights[0]
    for i in range(1, weights.shape[0]):
        whole = whole + weights[i]
    share = jnp.full((1, 128), weights[point].astype(F32), F32) / jnp.full(
        (1, 128), whole.astype(F32), F32
    )
    read = reader(first, second, far)
    for p in range(2):
        index, sign = side(p)
        for r in range(0, rows, CHUNK):
            now = slice(r, r + CHUNK)
            por = porosity[index, now]
            inverse = 1.0 / (QRAMP + por)
            alpha = (AMAX * QRAMP) * (1.0 - por) * inverse
            drive = jnp.where(flags[index, now] == 2, 1.0, 0.0) - alpha
            u = [vel[0, d, index, now].astype(F32) for d in range(3)]
            parts, _ = local_chunk(read, p, sign, r, CHUNK, rows, u, nu, scaled[p, now], drive)
            slope = (-AMAX * QRAMP * (1.0 + QRAMP)) * (inverse * inverse) * share
            for c in range(4):
                part[c, p, now] = parts[c]
            for c in range(3):
                pull[c, p, now] = slope * u[c]


def counts(at, whole):
    return 4.0 - jnp.where(at == 0, 1.0, 0.0) - jnp.where(at == whole - 1, 1.0, 0.0)


def second_join(
    part, factor, scaled, pull, first, second, far, state, mine, theirs, held, sens, sems
):
    rows = far.shape[1]
    read = reader(first, second, far)
    copies = []
    for p in range(2):
        index, sign = side(p)
        for r in range(0, rows, CHUNK):
            now = slice(r, r + CHUNK)
            halo = [read(c, p, r, CHUNK) for c in range(4)]
            lam0, mu = join_first(part, factor, scaled, (halo[0], halo[3]), p, sign, now)
            lam1, lam2 = join_second(part, factor, halo[1:3], p, now)
            held[p, 0, now] = lam0
            held[p, 1, now] = lam1
            held[p, 2, now] = lam2
            held[p, 3, now] = mu
            sens[p, now] = pull[0, p, now] * lam0 + pull[1, p, now] * lam1 + pull[2, p, now] * lam2
        copy = pltpu.make_async_copy(held.at[p], state.at[0, :, index], sems.at[p])
        copy.start()
        copies.append(copy)
    half = rows // 2
    core = lax.axis_index("core")
    lane = lax.broadcasted_iota(jnp.int32, (CHUNK, 128), 1)
    row = lax.broadcasted_iota(jnp.int32, (CHUNK, 128), 0)
    for p in range(2):
        index, _ = side(p)
        for r in range(0, rows, CHUNK):
            read = lambda a, n: sens[p, a : a + n]
            ym, yp = row_shift(read, r, CHUNK, rows)
            along = ym + yp + 2.0 * read(r, CHUNK)
            zm, zp = lane_shift(along)
            total = (zm + zp + 2.0 * along) / (counts(row + r, rows) * counts(lane, 128))
            owner = r // half
            to = slice(r - owner * half, r - owner * half + CHUNK)

            @pl.when(core == owner)
            def _():
                mine[index, to] = total

            @pl.when(core != owner)
            def _():
                theirs[index, to] = total

    for copy in copies:
        copy.wait()


def left_half(shape):
    return lax.broadcasted_iota(jnp.int32, shape, 1) < shape[1] // 2


def swap_halves(value):
    return pltpu.roll(value, value.shape[1] // 2, 1)


def interleave(one, two):
    left = left_half(one.shape)
    return jnp.where(left, one, swap_halves(two)), jnp.where(left, swap_halves(one), two)


def add_cores(mine, other, blocks):
    half = mine.shape[1]
    for r in range(0, half, CHUNK):
        now = slice(r, r + CHUNK)
        first, second = interleave(mine[0, now] + other[0, now], mine[1, now] + other[1, now])
        blocks[now] = first
        blocks[half + r : half + r + CHUNK] = second


def filter_planes(points, blocks, out):
    slabs = blocks.shape[0] // points
    total = blocks[pl.ds(0, slabs, stride=points)]
    for q in range(1, points):
        total = total + blocks[pl.ds(q, slabs, stride=points)]
    swapped = swap_halves(total)
    at = lax.broadcasted_iota(jnp.int32, total.shape, 0)
    left = left_half(total.shape)
    below = jnp.where(at == 0, 0.0, pltpu.roll(swapped, 1, 0))
    above = jnp.where(at == slabs - 1, 0.0, pltpu.roll(swapped, slabs - 1, 0))
    plane = 2 * at + jnp.where(left, 0, 1)
    filtered = (2.0 * total + swapped + jnp.where(left, below, above)) / counts(plane, 2 * slabs)
    largest = jnp.full(total.shape, jnp.max(jnp.abs(filtered)), F32)
    for q in range(points):
        out[pl.ds(2 * q, slabs, stride=2 * points)] = filtered
        out[pl.ds(2 * q + 1, slabs, stride=2 * points)] = largest


def update(porosity, own, other, out):
    n = own.shape[0] // 2
    half = n // 2
    ends = [ref[pl.ds(1, n, stride=2)] for ref in (own, other)]
    largest = jnp.max(jnp.maximum(ends[0], ends[1]))
    factor = STEP / jnp.full((1, 128), largest + EPS, F32)
    core = lax.axis_index("core")
    for held, base in ((own, core * half), (other, half - core * half)):
        for r in range(0, half, CHUNK):
            to = pl.ds(pl.multiple_of(base + r, CHUNK), CHUNK)
            first = held[pl.ds(2 * r, CHUNK, stride=2)]
            second = held[pl.ds(2 * (half + r), CHUNK, stride=2)]
            for p, moved in enumerate(interleave(first, second)):
                out[p, to] = jnp.clip(porosity[p, to] - factor * moved, 0.0, 1.0)


def shards(adjoint, fwd_velocity, reynolds, weights, porosity, flags):
    planes, rows, depth = porosity.shape
    points = lax.axis_size("zhi")
    cores = lax.axis_size("core")
    spaces = lax.axis_size("zlo") * lax.axis_size("x") * lax.axis_size("y")

    def pairs(start):
        there = [(i, i + 1) for i in range(start, spaces - 1, 2)]
        return there + [(j, i) for i, j in there]

    def swap(value, start):
        return lax.ppermute(value, SPACE, pairs(start))

    half_state = shape(4, planes, rows, depth)
    field = shape(planes, rows, depth)
    plane = shape(4, rows, depth)
    pair = shape(2, rows, depth)
    first, second, far = call(
        take_planes,
        [VM],
        [pair, pair, plane],
    )(adjoint)
    halo_first = swap(first, 1)
    halo_far = swap(far, 0)
    halo_second = swap(second, 1)
    part, factor, scaled = call(first_local, [SM] + [VM] * 6, [half_state, field, field])(
        reynolds, first, second, far, fwd_velocity, porosity, flags
    )
    (first,) = call(near_first, [VM] * 4, [pair])(part, factor, scaled, halo_first)
    halo_first = swap(first, 1)
    (far,) = call(far_all, [VM] * 5, [plane])(part, factor, scaled, halo_far, first)
    halo_far = swap(far, 0)
    (second,) = call(near_second, [VM] * 4, [pair])(part, factor, halo_second, far)
    halo_second = swap(second, 1)
    part, pull = call(
        second_local,
        [SM, SM] + [VM] * 7,
        [half_state, shape(3, planes, rows, depth)],
    )(reynolds, weights, first, second, far, fwd_velocity, porosity, flags, scaled)
    half = shape(planes, rows // cores, depth)
    state, mine, theirs = call(
        second_join,
        [VM] * 7,
        [shape(1, 4, planes, rows, depth), half, half],
        specs=[HB, VM, VM],
        scratch=[
            pltpu.VMEM((planes, 4, rows, depth), F32),
            pltpu.VMEM((planes, rows, depth), F32),
            pltpu.SemaphoreType.DMA((2,)),
        ],
    )(part, factor, scaled, pull, halo_first, halo_second, halo_far)
    other = lax.ppermute(theirs, "core", [(0, 1), (1, 0)])
    group = points * spaces
    (blocks,) = call(add_cores, [VM, VM], [shape(group, depth)])(mine, other)
    blocks = lax.all_to_all(blocks.reshape(group, 1, depth), SPACE + ("zhi",), 0, 0, tiled=True)
    (copies,) = call(functools.partial(filter_planes, points), [VM], [shape(2 * group, depth)])(
        blocks.reshape(group, depth)
    )
    own = lax.all_to_all(copies.reshape(group, 2, depth), SPACE + ("zhi",), 0, 0, tiled=True)
    own = own.reshape(2 * group, depth)
    other = lax.ppermute(own, "core", [(0, 1), (1, 0)])
    (porosity_new,) = call(update, [VM] * 3, [field])(porosity, own, other)
    return state, porosity_new


def solution(mesh):
    fine = Mesh(mesh.devices.reshape(4, 2, 4, 4, 4), POINT + SPACE)
    return jax.shard_map(
        shards,
        mesh=fine,
        in_specs=(
            P(POINT, None, SPACE, None, None),
            P(POINT, None, SPACE, None, None),
            P(POINT),
            P(),
            P(SPACE, None, None),
            P(SPACE, None, None),
        ),
        out_specs=(P(POINT, None, SPACE, None, None), P(SPACE, None, None)),
        check_vma=False,
    )
```

```python
import functools

import jax
import jax.numpy as jnp
from jax import lax
from jax.experimental import pallas as pl
from jax.experimental.pallas import tpu as pltpu
from jax.sharding import Mesh
from jax.sharding import PartitionSpec as P

AMAX = 50.0
QRAMP = 0.1
BETA = 0.5
STEP = 0.2
EPS = 1e-06

POINT = ("zhi", "core")
SPACE = ("zlo", "x", "y")
CHUNK = 32
VM = pl.BlockSpec(memory_space=pltpu.VMEM)
SM = pl.BlockSpec(memory_space=pltpu.SMEM)
HB = pl.BlockSpec(memory_space=pltpu.HBM)
F32 = jnp.float32


def shape(*dims):
    return jax.ShapeDtypeStruct(dims, F32)


def call(body, ins, outs, specs=None, scratch=(), vmem=32.0, flops=1_000_000):
    return pl.pallas_call(
        body,
        in_specs=ins,
        out_specs=[VM] * len(outs) if specs is None else specs,
        out_shape=list(outs),
        scratch_shapes=list(scratch),
        compiler_params=pltpu.CompilerParams(vmem_limit_bytes=int(vmem * 2**20)),
        cost_estimate=pl.CostEstimate(flops=flops, bytes_accessed=4_000_000, transcendentals=0),
    )


def row_shift(read, r, size, rows):
    at = lax.broadcasted_iota(jnp.int32, (size, 128), 0)
    if r == 0:
        before = jnp.where(at == 0, 0.0, pltpu.roll(read(0, size), 1, 0))
    else:
        before = read(r - 1, size)
    if r + size == rows:
        after = jnp.where(at == size - 1, 0.0, pltpu.roll(read(r, size), size - 1, 0))
    else:
        after = read(r + 1, size)
    return before, after


def lane_shift(value):
    at = lax.broadcasted_iota(jnp.int32, value.shape, 1)
    last = value.shape[1] - 1
    before = jnp.where(at == 0, 0.0, pltpu.roll(value, 1, 1))
    after = jnp.where(at == last, 0.0, pltpu.roll(value, last, 1))
    return before, after


def side(p):
    place = lax.axis_index("zlo") * lax.axis_size("x") + lax.axis_index("x")
    odd = lax.rem(place * lax.axis_size("y") + lax.axis_index("y"), 2)
    index = odd if p == 0 else 1 - odd
    return index, (1 - 2 * index).astype(F32)


def reader(first, second, far):
    def read(c, p, r, n):
        if p == 1:
            return far[c, r : r + n]
        if c in (1, 2):
            return second[c - 1, r : r + n]
        return first[min(c, 1), r : r + n]

    return read


def take_planes(adjoint, first, second, far):
    index, _ = side(0)
    for r in range(0, far.shape[1], CHUNK):
        now = slice(r, r + CHUNK)
        first[0, now] = adjoint[0, 0, index, now]
        first[1, now] = adjoint[0, 3, index, now]
        for c in range(2):
            second[c, now] = adjoint[0, c + 1, index, now]
        for c in range(4):
            far[c, now] = adjoint[0, c, 1 - index, now]


def local_chunk(read, p, sign, r, size, rows, u, nu, scale, drive):
    ux, uy, uz = [0.5 * v for v in u]
    inner = nu + sign * ux
    outer = nu - sign * ux
    y_after, y_before = nu + uy, nu - uy
    z_after, z_before = nu + uz, nu - uz
    mu = read(3, p, r, size)
    mu_in = read(3, 1 - p, r, size)
    mu_ym, mu_yp = row_shift(lambda a, n: read(3, p, a, n), r, size, rows)
    mu_zm, mu_zp = lane_shift(mu)
    gradient = [(0.5 * sign) * mu_in, 0.5 * (mu_yp - mu_ym), 0.5 * (mu_zp - mu_zm)]
    parts = []
    diverge = None
    for c in range(3):
        lam = read(c, p, r, size)
        lam_in = read(c, 1 - p, r, size)
        ym, yp = row_shift(lambda a, n: read(c, p, a, n), r, size, rows)
        zm, zp = lane_shift(lam)
        total = lam + inner * lam_in + y_after * yp + y_before * ym + z_after * zp + z_before * zm
        total = total - gradient[c] + u[c] * drive
        parts.append(scale * total)
        term = (sign * lam_in, yp - ym, zp - zm)[c]
        diverge = term if diverge is None else diverge + term
    parts.append(mu - (0.5 * BETA) * diverge)
    return parts, scale * outer


def viscosity_of(reynolds):
    return 20.0 / jnp.full((1, 128), reynolds[0], F32)


def first_local(reynolds, first, second, far, vel, porosity, flags, part, factor, scaled):
    rows = far.shape[1]
    nu = viscosity_of(reynolds)
    read = reader(first, second, far)
    for p in range(2):
        index, sign = side(p)
        for r in range(0, rows, CHUNK):
            now = slice(r, r + CHUNK)
            por = porosity[index, now]
            flag = flags[index, now]
            alpha = (AMAX * QRAMP) * (1.0 - por) / (QRAMP + por)
            scale = jnp.where(flag != 1, 1.0, 0.0) / (1.0 + 6.0 * nu + alpha)
            drive = jnp.where(flag == 2, 1.0, 0.0) - alpha
            u = [vel[0, d, index, now].astype(F32) for d in range(3)]
            parts, outer = local_chunk(read, p, sign, r, CHUNK, rows, u, nu, scale, drive)
            for c in range(4):
                part[c, p, now] = parts[c]
            factor[p, now] = outer
            scaled[p, now] = scale


def join_first(part, factor, scaled, halo, p, sign, now):
    lam, mu = halo
    outer = part[0, p, now] + factor[p, now] * lam + (0.5 * sign) * (scaled[p, now] * mu)
    return outer, part[3, p, now] + (0.5 * BETA * sign) * lam


def join_second(part, factor, halo, p, now):
    outer = factor[p, now]
    return [part[c + 1, p, now] + outer * halo[c] for c in range(2)]


def near_first(part, factor, scaled, halo, out):
    _, sign = side(0)
    for r in range(0, halo.shape[1], CHUNK):
        now = slice(r, r + CHUNK)
        out[0, now], out[1, now] = join_first(
            part, factor, scaled, (halo[0, now], halo[1, now]), 0, sign, now
        )


def near_second(part, factor, halo, after, out):
    for r in range(0, halo.shape[1], CHUNK):
        now = slice(r, r + CHUNK)
        out[0, now], out[1, now] = join_second(part, factor, (halo[0, now], halo[1, now]), 0, now)


def far_all(part, factor, scaled, halo, after, out):
    _, sign = side(1)
    for r in range(0, halo.shape[1], CHUNK):
        now = slice(r, r + CHUNK)
        out[0, now], out[3, now] = join_first(
            part, factor, scaled, (halo[0, now], halo[3, now]), 1, sign, now
        )
        out[1, now], out[2, now] = join_second(part, factor, (halo[1, now], halo[2, now]), 1, now)


def second_local(
    reynolds, weights, first, second, far, vel, porosity, flags, scaled, part, pull
):
    rows = far.shape[1]
    point = lax.axis_index("zhi") * lax.axis_size("core") + lax.axis_index("core")
    nu = viscosity_of(reynolds)
    whole = weights[0]
    for i in range(1, weights.shape[0]):
        whole = whole + weights[i]
    share = jnp.full((1, 128), weights[point].astype(F32), F32) / jnp.full(
        (1, 128), whole.astype(F32), F32
    )
    read = reader(first, second, far)
    for p in range(2):
        index, sign = side(p)
        for r in range(0, rows, CHUNK):
            now = slice(r, r + CHUNK)
            por = porosity[index, now]
            inverse = 1.0 / (QRAMP + por)
            alpha = (AMAX * QRAMP) * (1.0 - por) * inverse
            drive = jnp.where(flags[index, now] == 2, 1.0, 0.0) - alpha
            u = [vel[0, d, index, now].astype(F32) for d in range(3)]
            parts, _ = local_chunk(read, p, sign, r, CHUNK, rows, u, nu, scaled[p, now], drive)
            slope = (-AMAX * QRAMP * (1.0 + QRAMP)) * (inverse * inverse) * share
            for c in range(4):
                part[c, p, now] = parts[c]
            for c in range(3):
                pull[c, p, now] = slope * u[c]


def counts(at, whole):
    return 4.0 - jnp.where(at == 0, 1.0, 0.0) - jnp.where(at == whole - 1, 1.0, 0.0)


def second_join(
    part, factor, scaled, pull, first, second, far, state, mine, theirs, held, sens, weighted, sems
):
    rows = far.shape[1]
    read = reader(first, second, far)
    copies = []
    for p in range(2):
        index, sign = side(p)
        for r in range(0, rows, CHUNK):
            now = slice(r, r + CHUNK)
            halo = [read(c, p, r, CHUNK) for c in range(4)]
            lam0, mu = join_first(part, factor, scaled, (halo[0], halo[3]), p, sign, now)
            lam1, lam2 = join_second(part, factor, halo[1:3], p, now)
            held[p, 0, now] = lam0
            held[p, 1, now] = lam1
            held[p, 2, now] = lam2
            held[p, 3, now] = mu
            sens[p, now] = pull[0, p, now] * lam0 + pull[1, p, now] * lam1 + pull[2, p, now] * lam2
        copy = pltpu.make_async_copy(held.at[p], state.at[0, :, index], sems.at[p])
        copy.start()
        copies.append(copy)
    half = rows // 2
    core = lax.axis_index("core")
    lane = lax.broadcasted_iota(jnp.int32, (1, 128), 1)
    row = lax.broadcasted_iota(jnp.int32, (CHUNK, 128), 0)
    along_z = 1.0 / counts(lane, 128)
    inner = along_z * 0.25
    for p in range(2):
        index, _ = side(p)
        for r in range(0, rows, CHUNK):
            read = lambda a, n: sens[p, a : a + n]
            ym, yp = row_shift(read, r, CHUNK, rows)
            along = ym + yp + 2.0 * read(r, CHUNK)
            zm, zp = lane_shift(along)
            if r == 0 or r + CHUNK == rows:
                scale = along_z / counts(row + r, rows)
            else:
                scale = inner
            weighted[index, r : r + CHUNK] = (zm + zp + 2.0 * along) * scale
    for owner, (kept, sent) in enumerate(((0, half), (half, 0))):

        @pl.when(core == owner)
        def _():
            for p in range(2):
                mine[p] = weighted[p, kept : kept + half]
                theirs[p] = weighted[p, sent : sent + half]

    for copy in copies:
        copy.wait()


def left_half(shape):
    return lax.broadcasted_iota(jnp.int32, shape, 1) < shape[1] // 2


def swap_halves(value):
    return pltpu.roll(value, value.shape[1] // 2, 1)


def interleave(one, two):
    left = left_half(one.shape)
    return jnp.where(left, one, swap_halves(two)), jnp.where(left, swap_halves(one), two)


def add_cores(mine, other, blocks):
    half = mine.shape[1]
    for r in range(0, half, CHUNK):
        now = slice(r, r + CHUNK)
        first, second = interleave(mine[0, now] + other[0, now], mine[1, now] + other[1, now])
        blocks[now] = first
        blocks[half + r : half + r + CHUNK] = second


def filter_planes(points, blocks, out):
    slabs = blocks.shape[0] // points
    total = blocks[pl.ds(0, slabs, stride=points)]
    for q in range(1, points):
        total = total + blocks[pl.ds(q, slabs, stride=points)]
    swapped = swap_halves(total)
    at = lax.broadcasted_iota(jnp.int32, total.shape, 0)
    left = left_half(total.shape)
    below = jnp.where(at == 0, 0.0, pltpu.roll(swapped, 1, 0))
    above = jnp.where(at == slabs - 1, 0.0, pltpu.roll(swapped, slabs - 1, 0))
    plane = 2 * at + jnp.where(left, 0, 1)
    filtered = (2.0 * total + swapped + jnp.where(left, below, above)) / counts(plane, 2 * slabs)
    largest = jnp.full(total.shape, jnp.max(jnp.abs(filtered)), F32)
    for q in range(points):
        out[pl.ds(2 * q, slabs, stride=2 * points)] = filtered
        out[pl.ds(2 * q + 1, slabs, stride=2 * points)] = largest


def update(porosity, own, other, out):
    n = own.shape[0] // 2
    half = n // 2
    ends = [ref[pl.ds(1, n, stride=2)] for ref in (own, other)]
    largest = jnp.max(jnp.maximum(ends[0], ends[1]))
    factor = STEP / jnp.full((1, 128), largest + EPS, F32)
    core = lax.axis_index("core")
    for held, base in ((own, core * half), (other, half - core * half)):
        for r in range(0, half, CHUNK):
            to = pl.ds(pl.multiple_of(base + r, CHUNK), CHUNK)
            first = held[pl.ds(2 * r, CHUNK, stride=2)]
            second = held[pl.ds(2 * (half + r), CHUNK, stride=2)]
            for p, moved in enumerate(interleave(first, second)):
                out[p, to] = jnp.clip(porosity[p, to] - factor * moved, 0.0, 1.0)


def shards(adjoint, fwd_velocity, reynolds, weights, porosity, flags):
    planes, rows, depth = porosity.shape
    points = lax.axis_size("zhi")
    cores = lax.axis_size("core")
    spaces = lax.axis_size("zlo") * lax.axis_size("x") * lax.axis_size("y")

    def pairs(start):
        there = [(i, i + 1) for i in range(start, spaces - 1, 2)]
        return there + [(j, i) for i, j in there]

    def swap(value, start):
        return lax.ppermute(value, SPACE, pairs(start))

    half_state = shape(4, planes, rows, depth)
    field = shape(planes, rows, depth)
    plane = shape(4, rows, depth)
    pair = shape(2, rows, depth)
    first, second, far = call(
        take_planes,
        [VM],
        [pair, pair, plane],
    )(adjoint)
    halo_first = swap(first, 1)
    halo_far = swap(far, 0)
    halo_second = swap(second, 1)
    part, factor, scaled = call(first_local, [SM] + [VM] * 6, [half_state, field, field], flops=1000000)(
        reynolds, first, second, far, fwd_velocity, porosity, flags
    )
    (first,) = call(near_first, [VM] * 4, [pair], flops=4000000000)(part, factor, scaled, halo_first)
    halo_first = swap(first, 1)
    (far,) = call(far_all, [VM] * 5, [plane], flops=4000000000)(part, factor, scaled, halo_far, first)
    halo_far = swap(far, 0)
    (second,) = call(near_second, [VM] * 4, [pair], flops=4000000000)(part, factor, halo_second, far)
    halo_second = swap(second, 1)
    part, pull = call(
        second_local,
        [SM, SM] + [VM] * 7,
        [half_state, shape(3, planes, rows, depth)],
        flops=4000000000,
    )(reynolds, weights, first, second, far, fwd_velocity, porosity, flags, scaled)
    half = shape(planes, rows // cores, depth)
    state, mine, theirs = call(
        second_join,
        [VM] * 7,
        [shape(1, 4, planes, rows, depth), half, half],
        specs=[HB, VM, VM],
        scratch=[
            pltpu.VMEM((planes, 4, rows, depth), F32),
            pltpu.VMEM((planes, rows, depth), F32),
            pltpu.VMEM((planes, rows, depth), F32),
            pltpu.SemaphoreType.DMA((2,)),
        ],
    )(part, factor, scaled, pull, halo_first, halo_second, halo_far)
    other = lax.ppermute(theirs, "core", [(0, 1), (1, 0)])
    group = points * spaces
    (blocks,) = call(add_cores, [VM, VM], [shape(group, depth)])(mine, other)
    blocks = lax.all_to_all(blocks.reshape(group, 1, depth), SPACE + ("zhi",), 0, 0, tiled=True)
    (copies,) = call(functools.partial(filter_planes, points), [VM], [shape(2 * group, depth)])(
        blocks.reshape(group, depth)
    )
    own = lax.all_to_all(copies.reshape(group, 2, depth), SPACE + ("zhi",), 0, 0, tiled=True)
    own = own.reshape(2 * group, depth)
    other = lax.ppermute(own, "core", [(0, 1), (1, 0)])
    (porosity_new,) = call(update, [VM] * 3, [field])(porosity, own, other)
    return state, porosity_new


def solution(mesh):
    fine = Mesh(mesh.devices.reshape(4, 2, 4, 4, 4), POINT + SPACE)
    return jax.shard_map(
        shards,
        mesh=fine,
        in_specs=(
            P(POINT, None, SPACE, None, None),
            P(POINT, None, SPACE, None, None),
            P(POINT),
            P(),
            P(SPACE, None, None),
            P(SPACE, None, None),
        ),
        out_specs=(P(POINT, None, SPACE, None, None), P(SPACE, None, None)),
        check_vma=False,
    )
```

```python
import functools

import jax
import jax.numpy as jnp
from jax import lax
from jax.experimental import pallas as pl
from jax.experimental.pallas import tpu as pltpu
from jax.sharding import Mesh
from jax.sharding import PartitionSpec as P

AMAX = 50.0
QRAMP = 0.1
BETA = 0.5
STEP = 0.2
EPS = 1e-06

POINT = ("zhi", "core")
SPACE = ("zlo", "x", "y")
CHUNK = 32
VM = pl.BlockSpec(memory_space=pltpu.VMEM)
SM = pl.BlockSpec(memory_space=pltpu.SMEM)
HB = pl.BlockSpec(memory_space=pltpu.HBM)
F32 = jnp.float32


def shape(*dims):
    return jax.ShapeDtypeStruct(dims, F32)


def call(body, ins, outs, specs=None, scratch=(), vmem=32.0, flops=1_000_000):
    return pl.pallas_call(
        body,
        in_specs=ins,
        out_specs=[VM] * len(outs) if specs is None else specs,
        out_shape=list(outs),
        scratch_shapes=list(scratch),
        compiler_params=pltpu.CompilerParams(vmem_limit_bytes=int(vmem * 2**20)),
        cost_estimate=pl.CostEstimate(flops=flops, bytes_accessed=4_000_000, transcendentals=0),
    )


def row_shift(read, r, size, rows):
    at = lax.broadcasted_iota(jnp.int32, (size, 128), 0)
    if r == 0:
        before = jnp.where(at == 0, 0.0, pltpu.roll(read(0, size), 1, 0))
    else:
        before = read(r - 1, size)
    if r + size == rows:
        after = jnp.where(at == size - 1, 0.0, pltpu.roll(read(r, size), size - 1, 0))
    else:
        after = read(r + 1, size)
    return before, after


def lane_shift(value):
    at = lax.broadcasted_iota(jnp.int32, value.shape, 1)
    last = value.shape[1] - 1
    before = jnp.where(at == 0, 0.0, pltpu.roll(value, 1, 1))
    after = jnp.where(at == last, 0.0, pltpu.roll(value, last, 1))
    return before, after


def side(p):
    place = lax.axis_index("zlo") * lax.axis_size("x") + lax.axis_index("x")
    odd = lax.rem(place * lax.axis_size("y") + lax.axis_index("y"), 2)
    index = odd if p == 0 else 1 - odd
    return index, (1 - 2 * index).astype(F32)


def reader(first, second, far):
    def read(c, p, r, n):
        if p == 1:
            return far[c, r : r + n]
        if c in (1, 2):
            return second[c - 1, r : r + n]
        return first[min(c, 1), r : r + n]

    return read


def take_planes(adjoint, first, second, far):
    index, _ = side(0)
    for r in range(0, far.shape[1], CHUNK):
        now = slice(r, r + CHUNK)
        first[0, now] = adjoint[0, 0, index, now]
        first[1, now] = adjoint[0, 3, index, now]
        for c in range(2):
            second[c, now] = adjoint[0, c + 1, index, now]
        for c in range(4):
            far[c, now] = adjoint[0, c, 1 - index, now]


def local_chunk(read, p, sign, r, size, rows, u, nu, scale, drive):
    ux, uy, uz = [0.5 * v for v in u]
    inner = nu + sign * ux
    outer = nu - sign * ux
    y_after, y_before = nu + uy, nu - uy
    z_after, z_before = nu + uz, nu - uz
    mu = read(3, p, r, size)
    mu_in = read(3, 1 - p, r, size)
    mu_ym, mu_yp = row_shift(lambda a, n: read(3, p, a, n), r, size, rows)
    mu_zm, mu_zp = lane_shift(mu)
    gradient = [(0.5 * sign) * mu_in, 0.5 * (mu_yp - mu_ym), 0.5 * (mu_zp - mu_zm)]
    parts = []
    diverge = None
    for c in range(3):
        lam = read(c, p, r, size)
        lam_in = read(c, 1 - p, r, size)
        ym, yp = row_shift(lambda a, n: read(c, p, a, n), r, size, rows)
        zm, zp = lane_shift(lam)
        total = lam + inner * lam_in + y_after * yp + y_before * ym + z_after * zp + z_before * zm
        total = total - gradient[c] + u[c] * drive
        parts.append(scale * total)
        term = (sign * lam_in, yp - ym, zp - zm)[c]
        diverge = term if diverge is None else diverge + term
    parts.append(mu - (0.5 * BETA) * diverge)
    return parts, scale * outer


def viscosity_of(reynolds):
    return 20.0 / jnp.full((1, 128), reynolds[0], F32)


def first_local(reynolds, first, second, far, vel, porosity, flags, part, factor, scaled):
    rows = far.shape[1]
    nu = viscosity_of(reynolds)
    read = reader(first, second, far)
    for p in range(2):
        index, sign = side(p)
        for r in range(0, rows, CHUNK):
            now = slice(r, r + CHUNK)
            por = porosity[index, now]
            flag = flags[index, now]
            alpha = (AMAX * QRAMP) * (1.0 - por) / (QRAMP + por)
            scale = jnp.where(flag != 1, 1.0, 0.0) / (1.0 + 6.0 * nu + alpha)
            drive = jnp.where(flag == 2, 1.0, 0.0) - alpha
            u = [vel[0, d, index, now].astype(F32) for d in range(3)]
            parts, outer = local_chunk(read, p, sign, r, CHUNK, rows, u, nu, scale, drive)
            for c in range(4):
                part[c, p, now] = parts[c]
            factor[p, now] = outer
            scaled[p, now] = scale


def join_first(part, factor, scaled, halo, p, sign, now):
    lam, mu = halo
    outer = part[0, p, now] + factor[p, now] * lam + (0.5 * sign) * (scaled[p, now] * mu)
    return outer, part[3, p, now] + (0.5 * BETA * sign) * lam


def join_second(part, factor, halo, p, now):
    outer = factor[p, now]
    return [part[c + 1, p, now] + outer * halo[c] for c in range(2)]


def near_first(part, factor, scaled, halo, out):
    _, sign = side(0)
    for r in range(0, halo.shape[1], CHUNK):
        now = slice(r, r + CHUNK)
        out[0, now], out[1, now] = join_first(
            part, factor, scaled, (halo[0, now], halo[1, now]), 0, sign, now
        )


def near_second(part, factor, halo, after, out):
    for r in range(0, halo.shape[1], CHUNK):
        now = slice(r, r + CHUNK)
        out[0, now], out[1, now] = join_second(part, factor, (halo[0, now], halo[1, now]), 0, now)


def far_all(part, factor, scaled, halo, after, out):
    _, sign = side(1)
    for r in range(0, halo.shape[1], CHUNK):
        now = slice(r, r + CHUNK)
        out[0, now], out[3, now] = join_first(
            part, factor, scaled, (halo[0, now], halo[3, now]), 1, sign, now
        )
        out[1, now], out[2, now] = join_second(part, factor, (halo[1, now], halo[2, now]), 1, now)


def second_local(
    reynolds, weights, first, second, far, vel, porosity, flags, scaled, part, pull
):
    rows = far.shape[1]
    point = lax.axis_index("zhi") * lax.axis_size("core") + lax.axis_index("core")
    nu = viscosity_of(reynolds)
    whole = weights[0]
    for i in range(1, weights.shape[0]):
        whole = whole + weights[i]
    share = jnp.full((1, 128), weights[point].astype(F32), F32) / jnp.full(
        (1, 128), whole.astype(F32), F32
    )
    read = reader(first, second, far)
    for p in range(2):
        index, sign = side(p)
        for r in range(0, rows, CHUNK):
            now = slice(r, r + CHUNK)
            por = porosity[index, now]
            inverse = 1.0 / (QRAMP + por)
            alpha = (AMAX * QRAMP) * (1.0 - por) * inverse
            drive = jnp.where(flags[index, now] == 2, 1.0, 0.0) - alpha
            u = [vel[0, d, index, now].astype(F32) for d in range(3)]
            parts, _ = local_chunk(read, p, sign, r, CHUNK, rows, u, nu, scaled[p, now], drive)
            slope = (-AMAX * QRAMP * (1.0 + QRAMP)) * (inverse * inverse) * share
            for c in range(4):
                part[c, p, now] = parts[c]
            for c in range(3):
                pull[c, p, now] = slope * u[c]


def counts(at, whole):
    return 4.0 - jnp.where(at == 0, 1.0, 0.0) - jnp.where(at == whole - 1, 1.0, 0.0)


def second_join(
    part, factor, scaled, pull, first, second, far, held, mine, theirs, sens, weighted
):
    rows = far.shape[1]
    read = reader(first, second, far)
    for p in range(2):
        _, sign = side(p)
        for r in range(0, rows, CHUNK):
            now = slice(r, r + CHUNK)
            halo = [read(c, p, r, CHUNK) for c in range(4)]
            lam0, mu = join_first(part, factor, scaled, (halo[0], halo[3]), p, sign, now)
            lam1, lam2 = join_second(part, factor, halo[1:3], p, now)
            held[p, 0, now] = lam0
            held[p, 1, now] = lam1
            held[p, 2, now] = lam2
            held[p, 3, now] = mu
            sens[p, now] = pull[0, p, now] * lam0 + pull[1, p, now] * lam1 + pull[2, p, now] * lam2
    half = rows // 2
    core = lax.axis_index("core")
    lane = lax.broadcasted_iota(jnp.int32, (1, 128), 1)
    row = lax.broadcasted_iota(jnp.int32, (CHUNK, 128), 0)
    along_z = 1.0 / counts(lane, 128)
    inner = along_z * 0.25
    for p in range(2):
        index, _ = side(p)
        for r in range(0, rows, CHUNK):
            read = lambda a, n: sens[p, a : a + n]
            ym, yp = row_shift(read, r, CHUNK, rows)
            along = ym + yp + 2.0 * read(r, CHUNK)
            zm, zp = lane_shift(along)
            if r == 0 or r + CHUNK == rows:
                scale = along_z / counts(row + r, rows)
            else:
                scale = inner
            weighted[index, r : r + CHUNK] = (zm + zp + 2.0 * along) * scale
    for owner, (kept, sent) in enumerate(((0, half), (half, 0))):

        @pl.when(core == owner)
        def _():
            for p in range(2):
                mine[p] = weighted[p, kept : kept + half]
                theirs[p] = weighted[p, sent : sent + half]


def write_state(held, state, sems):
    copies = [
        pltpu.make_async_copy(held.at[p], state.at[0, :, side(p)[0]], sems.at[p]) for p in range(2)
    ]
    for copy in copies:
        copy.start()
    for copy in copies:
        copy.wait()


def left_half(shape):
    return lax.broadcasted_iota(jnp.int32, shape, 1) < shape[1] // 2


def swap_halves(value):
    return pltpu.roll(value, value.shape[1] // 2, 1)


def interleave(one, two):
    left = left_half(one.shape)
    return jnp.where(left, one, swap_halves(two)), jnp.where(left, swap_halves(one), two)


def add_cores(mine, other, blocks):
    half = mine.shape[1]
    for r in range(0, half, CHUNK):
        now = slice(r, r + CHUNK)
        first, second = interleave(mine[0, now] + other[0, now], mine[1, now] + other[1, now])
        blocks[now] = first
        blocks[half + r : half + r + CHUNK] = second


def filter_planes(points, blocks, out):
    slabs = blocks.shape[0] // points
    total = blocks[pl.ds(0, slabs, stride=points)]
    for q in range(1, points):
        total = total + blocks[pl.ds(q, slabs, stride=points)]
    swapped = swap_halves(total)
    at = lax.broadcasted_iota(jnp.int32, total.shape, 0)
    left = left_half(total.shape)
    below = jnp.where(at == 0, 0.0, pltpu.roll(swapped, 1, 0))
    above = jnp.where(at == slabs - 1, 0.0, pltpu.roll(swapped, slabs - 1, 0))
    plane = 2 * at + jnp.where(left, 0, 1)
    filtered = (2.0 * total + swapped + jnp.where(left, below, above)) / counts(plane, 2 * slabs)
    largest = jnp.full(total.shape, jnp.max(jnp.abs(filtered)), F32)
    for q in range(points):
        out[pl.ds(2 * q, slabs, stride=2 * points)] = filtered
        out[pl.ds(2 * q + 1, slabs, stride=2 * points)] = largest


def update(porosity, own, other, out):
    n = own.shape[0] // 2
    half = n // 2
    ends = [ref[pl.ds(1, n, stride=2)] for ref in (own, other)]
    largest = jnp.max(jnp.maximum(ends[0], ends[1]))
    factor = STEP / jnp.full((1, 128), largest + EPS, F32)
    core = lax.axis_index("core")
    for held, base in ((own, core * half), (other, half - core * half)):
        for r in range(0, half, CHUNK):
            to = pl.ds(pl.multiple_of(base + r, CHUNK), CHUNK)
            first = held[pl.ds(2 * r, CHUNK, stride=2)]
            second = held[pl.ds(2 * (half + r), CHUNK, stride=2)]
            for p, moved in enumerate(interleave(first, second)):
                out[p, to] = jnp.clip(porosity[p, to] - factor * moved, 0.0, 1.0)


def shards(adjoint, fwd_velocity, reynolds, weights, porosity, flags):
    planes, rows, depth = porosity.shape
    points = lax.axis_size("zhi")
    cores = lax.axis_size("core")
    spaces = lax.axis_size("zlo") * lax.axis_size("x") * lax.axis_size("y")

    def pairs(start):
        there = [(i, i + 1) for i in range(start, spaces - 1, 2)]
        return there + [(j, i) for i, j in there]

    def swap(value, start):
        return lax.ppermute(value, SPACE, pairs(start))

    half_state = shape(4, planes, rows, depth)
    field = shape(planes, rows, depth)
    plane = shape(4, rows, depth)
    pair = shape(2, rows, depth)
    first, second, far = call(
        take_planes,
        [VM],
        [pair, pair, plane],
    )(adjoint)
    halo_first = swap(first, 1)
    halo_far = swap(far, 0)
    halo_second = swap(second, 1)
    part, factor, scaled = call(first_local, [SM] + [VM] * 6, [half_state, field, field], flops=1000000)(
        reynolds, first, second, far, fwd_velocity, porosity, flags
    )
    (first,) = call(near_first, [VM] * 4, [pair], flops=4000000000)(part, factor, scaled, halo_first)
    halo_first = swap(first, 1)
    (far,) = call(far_all, [VM] * 5, [plane], flops=4000000000)(part, factor, scaled, halo_far, first)
    halo_far = swap(far, 0)
    (second,) = call(near_second, [VM] * 4, [pair], flops=4000000000)(part, factor, halo_second, far)
    halo_second = swap(second, 1)
    part, pull = call(
        second_local,
        [SM, SM] + [VM] * 7,
        [half_state, shape(3, planes, rows, depth)],
        flops=4000000000,
    )(reynolds, weights, first, second, far, fwd_velocity, porosity, flags, scaled)
    half = shape(planes, rows // cores, depth)
    held, mine, theirs = call(
        second_join,
        [VM] * 7,
        [shape(planes, 4, rows, depth), half, half],
        scratch=[pltpu.VMEM((planes, rows, depth), F32)] * 2,
    )(part, factor, scaled, pull, halo_first, halo_second, halo_far)
    other = lax.ppermute(theirs, "core", [(0, 1), (1, 0)])
    (state,) = call(
        write_state,
        [VM],
        [shape(1, 4, planes, rows, depth)],
        specs=[HB],
        scratch=[pltpu.SemaphoreType.DMA((2,))],
    )(held)
    group = points * spaces
    (blocks,) = call(add_cores, [VM, VM], [shape(group, depth)])(mine, other)
    blocks = lax.all_to_all(blocks.reshape(group, 1, depth), SPACE + ("zhi",), 0, 0, tiled=True)
    (copies,) = call(functools.partial(filter_planes, points), [VM], [shape(2 * group, depth)])(
        blocks.reshape(group, depth)
    )
    own = lax.all_to_all(copies.reshape(group, 2, depth), SPACE + ("zhi",), 0, 0, tiled=True)
    own = own.reshape(2 * group, depth)
    other = lax.ppermute(own, "core", [(0, 1), (1, 0)])
    (porosity_new,) = call(update, [VM] * 3, [field])(porosity, own, other)
    return state, porosity_new


def solution(mesh):
    fine = Mesh(mesh.devices.reshape(4, 2, 4, 4, 4), POINT + SPACE)
    return jax.shard_map(
        shards,
        mesh=fine,
        in_specs=(
            P(POINT, None, SPACE, None, None),
            P(POINT, None, SPACE, None, None),
            P(POINT),
            P(),
            P(SPACE, None, None),
            P(SPACE, None, None),
        ),
        out_specs=(P(POINT, None, SPACE, None, None), P(SPACE, None, None)),
        check_vma=False,
    )
```

```python
import functools

import jax
import jax.numpy as jnp
from jax import lax
from jax.experimental import pallas as pl
from jax.experimental.pallas import tpu as pltpu
from jax.sharding import Mesh
from jax.sharding import PartitionSpec as P

AMAX = 50.0
QRAMP = 0.1
BETA = 0.5
STEP = 0.2
EPS = 1e-06

POINT = ("zhi", "core")
SPACE = ("zlo", "x", "y")
CHUNK = 32
VM = pl.BlockSpec(memory_space=pltpu.VMEM)
SM = pl.BlockSpec(memory_space=pltpu.SMEM)
HB = pl.BlockSpec(memory_space=pltpu.HBM)
F32 = jnp.float32


def shape(*dims):
    return jax.ShapeDtypeStruct(dims, F32)


def call(body, ins, outs, specs=None, scratch=(), vmem=32.0, flops=1_000_000):
    return pl.pallas_call(
        body,
        in_specs=ins,
        out_specs=[VM] * len(outs) if specs is None else specs,
        out_shape=list(outs),
        scratch_shapes=list(scratch),
        compiler_params=pltpu.CompilerParams(vmem_limit_bytes=int(vmem * 2**20)),
        cost_estimate=pl.CostEstimate(flops=flops, bytes_accessed=4_000_000, transcendentals=0),
    )


def row_shift(read, r, size, rows):
    at = lax.broadcasted_iota(jnp.int32, (size, 128), 0)
    if r == 0:
        before = jnp.where(at == 0, 0.0, pltpu.roll(read(0, size), 1, 0))
    else:
        before = read(r - 1, size)
    if r + size == rows:
        after = jnp.where(at == size - 1, 0.0, pltpu.roll(read(r, size), size - 1, 0))
    else:
        after = read(r + 1, size)
    return before, after


def lane_shift(value):
    at = lax.broadcasted_iota(jnp.int32, value.shape, 1)
    last = value.shape[1] - 1
    before = jnp.where(at == 0, 0.0, pltpu.roll(value, 1, 1))
    after = jnp.where(at == last, 0.0, pltpu.roll(value, last, 1))
    return before, after


def side(p):
    place = lax.axis_index("zlo") * lax.axis_size("x") + lax.axis_index("x")
    odd = lax.rem(place * lax.axis_size("y") + lax.axis_index("y"), 2)
    index = odd if p == 0 else 1 - odd
    return index, (1 - 2 * index).astype(F32)


def reader(first, second, far):
    def read(c, p, r, n):
        if p == 1:
            return far[c, r : r + n]
        if c in (1, 2):
            return second[c - 1, r : r + n]
        return first[min(c, 1), r : r + n]

    return read


def take_planes(adjoint, first, second, far):
    index, _ = side(0)
    for r in range(0, far.shape[1], CHUNK):
        now = slice(r, r + CHUNK)
        first[0, now] = adjoint[0, 0, index, now]
        first[1, now] = adjoint[0, 3, index, now]
        for c in range(2):
            second[c, now] = adjoint[0, c + 1, index, now]
        for c in range(4):
            far[c, now] = adjoint[0, c, 1 - index, now]


def local_chunk(read, p, sign, r, size, rows, u, nu, scale, drive):
    ux, uy, uz = [0.5 * v for v in u]
    inner = nu + sign * ux
    outer = nu - sign * ux
    y_after, y_before = nu + uy, nu - uy
    z_after, z_before = nu + uz, nu - uz
    mu = read(3, p, r, size)
    mu_in = read(3, 1 - p, r, size)
    mu_ym, mu_yp = row_shift(lambda a, n: read(3, p, a, n), r, size, rows)
    mu_zm, mu_zp = lane_shift(mu)
    gradient = [(0.5 * sign) * mu_in, 0.5 * (mu_yp - mu_ym), 0.5 * (mu_zp - mu_zm)]
    parts = []
    diverge = None
    for c in range(3):
        lam = read(c, p, r, size)
        lam_in = read(c, 1 - p, r, size)
        ym, yp = row_shift(lambda a, n: read(c, p, a, n), r, size, rows)
        zm, zp = lane_shift(lam)
        total = lam + inner * lam_in + y_after * yp + y_before * ym + z_after * zp + z_before * zm
        total = total - gradient[c] + u[c] * drive
        parts.append(scale * total)
        term = (sign * lam_in, yp - ym, zp - zm)[c]
        diverge = term if diverge is None else diverge + term
    parts.append(mu - (0.5 * BETA) * diverge)
    return parts, scale * outer


def viscosity_of(reynolds):
    return 20.0 / jnp.full((1, 128), reynolds[0], F32)


def first_local(reynolds, first, second, far, vel, porosity, flags, part, factor, scaled):
    rows = far.shape[1]
    nu = viscosity_of(reynolds)
    read = reader(first, second, far)
    for p in range(2):
        index, sign = side(p)
        for r in range(0, rows, CHUNK):
            now = slice(r, r + CHUNK)
            por = porosity[index, now]
            flag = flags[index, now]
            alpha = (AMAX * QRAMP) * (1.0 - por) / (QRAMP + por)
            scale = jnp.where(flag != 1, 1.0, 0.0) / (1.0 + 6.0 * nu + alpha)
            drive = jnp.where(flag == 2, 1.0, 0.0) - alpha
            u = [vel[0, d, index, now].astype(F32) for d in range(3)]
            parts, outer = local_chunk(read, p, sign, r, CHUNK, rows, u, nu, scale, drive)
            for c in range(4):
                part[c, p, now] = parts[c]
            factor[p, now] = outer
            scaled[p, now] = scale


def join_first(part, factor, scaled, halo, p, sign, now):
    lam, mu = halo
    outer = part[0, p, now] + factor[p, now] * lam + (0.5 * sign) * (scaled[p, now] * mu)
    return outer, part[3, p, now] + (0.5 * BETA * sign) * lam


def join_second(part, factor, halo, p, now):
    outer = factor[p, now]
    return [part[c + 1, p, now] + outer * halo[c] for c in range(2)]


def near_first(part, factor, scaled, halo, out):
    _, sign = side(0)
    for r in range(0, halo.shape[1], CHUNK):
        now = slice(r, r + CHUNK)
        out[0, now], out[1, now] = join_first(
            part, factor, scaled, (halo[0, now], halo[1, now]), 0, sign, now
        )


def near_second(part, factor, halo, after, out):
    for r in range(0, halo.shape[1], CHUNK):
        now = slice(r, r + CHUNK)
        out[0, now], out[1, now] = join_second(part, factor, (halo[0, now], halo[1, now]), 0, now)


def far_all(part, factor, scaled, halo, after, out):
    _, sign = side(1)
    for r in range(0, halo.shape[1], CHUNK):
        now = slice(r, r + CHUNK)
        out[0, now], out[3, now] = join_first(
            part, factor, scaled, (halo[0, now], halo[3, now]), 1, sign, now
        )
        out[1, now], out[2, now] = join_second(part, factor, (halo[1, now], halo[2, now]), 1, now)


def second_local(
    reynolds, weights, first, second, far, vel, porosity, flags, scaled, part, pull
):
    rows = far.shape[1]
    point = lax.axis_index("zhi") * lax.axis_size("core") + lax.axis_index("core")
    nu = viscosity_of(reynolds)
    whole = weights[0]
    for i in range(1, weights.shape[0]):
        whole = whole + weights[i]
    share = jnp.full((1, 128), weights[point].astype(F32), F32) / jnp.full(
        (1, 128), whole.astype(F32), F32
    )
    read = reader(first, second, far)
    for p in range(2):
        index, sign = side(p)
        for r in range(0, rows, CHUNK):
            now = slice(r, r + CHUNK)
            por = porosity[index, now]
            inverse = 1.0 / (QRAMP + por)
            alpha = (AMAX * QRAMP) * (1.0 - por) * inverse
            drive = jnp.where(flags[index, now] == 2, 1.0, 0.0) - alpha
            u = [vel[0, d, index, now].astype(F32) for d in range(3)]
            parts, _ = local_chunk(read, p, sign, r, CHUNK, rows, u, nu, scaled[p, now], drive)
            slope = (-AMAX * QRAMP * (1.0 + QRAMP)) * (inverse * inverse) * share
            for c in range(4):
                part[c, p, now] = parts[c]
            for c in range(3):
                pull[c, p, now] = slope * u[c]


def counts(at, whole):
    return 4.0 - jnp.where(at == 0, 1.0, 0.0) - jnp.where(at == whole - 1, 1.0, 0.0)


def second_join(
    part, factor, scaled, pull, first, second, far, held, mine, theirs, sens, weighted
):
    rows = far.shape[1]
    read = reader(first, second, far)
    for p in range(2):
        _, sign = side(p)
        for r in range(0, rows, CHUNK):
            now = slice(r, r + CHUNK)
            halo = [read(c, p, r, CHUNK) for c in range(4)]
            lam0, mu = join_first(part, factor, scaled, (halo[0], halo[3]), p, sign, now)
            lam1, lam2 = join_second(part, factor, halo[1:3], p, now)
            held[p, 0, now] = lam0
            held[p, 1, now] = lam1
            held[p, 2, now] = lam2
            held[p, 3, now] = mu
            sens[p, now] = pull[0, p, now] * lam0 + pull[1, p, now] * lam1 + pull[2, p, now] * lam2
    half = rows // 2
    core = lax.axis_index("core")
    lane = lax.broadcasted_iota(jnp.int32, (1, 128), 1)
    row = lax.broadcasted_iota(jnp.int32, (CHUNK, 128), 0)
    along_z = 1.0 / counts(lane, 128)
    inner = along_z * 0.25
    for p in range(2):
        index, _ = side(p)
        for r in range(0, rows, CHUNK):
            read = lambda a, n: sens[p, a : a + n]
            ym, yp = row_shift(read, r, CHUNK, rows)
            along = ym + yp + 2.0 * read(r, CHUNK)
            zm, zp = lane_shift(along)
            if r == 0 or r + CHUNK == rows:
                scale = along_z / counts(row + r, rows)
            else:
                scale = inner
            weighted[index, r : r + CHUNK] = (zm + zp + 2.0 * along) * scale
    for owner, (kept, sent) in enumerate(((0, half), (half, 0))):

        @pl.when(core == owner)
        def _():
            for p in range(2):
                mine[p] = weighted[p, kept : kept + half]
                theirs[p] = weighted[p, sent : sent + half]


def write_state(held, state, sems):
    copies = [
        pltpu.make_async_copy(held.at[p], state.at[0, :, side(p)[0]], sems.at[p]) for p in range(2)
    ]
    for copy in copies:
        copy.start()
    for copy in copies:
        copy.wait()


def left_half(shape):
    return lax.broadcasted_iota(jnp.int32, shape, 1) < shape[1] // 2


def swap_halves(value):
    return pltpu.roll(value, value.shape[1] // 2, 1)


def interleave(one, two):
    left = left_half(one.shape)
    return jnp.where(left, one, swap_halves(two)), jnp.where(left, swap_halves(one), two)


def add_cores(mine, other, blocks):
    half = mine.shape[1]
    for r in range(0, half, CHUNK):
        now = slice(r, r + CHUNK)
        first, second = interleave(mine[0, now] + other[0, now], mine[1, now] + other[1, now])
        blocks[now] = first
        blocks[half + r : half + r + CHUNK] = second


def filter_planes(points, blocks, out):
    slabs = blocks.shape[0] // points
    total = blocks[pl.ds(0, slabs, stride=points)]
    for q in range(1, points):
        total = total + blocks[pl.ds(q, slabs, stride=points)]
    swapped = swap_halves(total)
    at = lax.broadcasted_iota(jnp.int32, total.shape, 0)
    left = left_half(total.shape)
    below = jnp.where(at == 0, 0.0, pltpu.roll(swapped, 1, 0))
    above = jnp.where(at == slabs - 1, 0.0, pltpu.roll(swapped, slabs - 1, 0))
    plane = 2 * at + jnp.where(left, 0, 1)
    filtered = (2.0 * total + swapped + jnp.where(left, below, above)) / counts(plane, 2 * slabs)
    largest = jnp.broadcast_to(jnp.max(jnp.abs(filtered), axis=0, keepdims=True), total.shape)
    for q in range(points):
        out[pl.ds(2 * q, slabs, stride=2 * points)] = filtered
        out[pl.ds(2 * q + 1, slabs, stride=2 * points)] = largest


def update(porosity, own, other, out):
    n = own.shape[0] // 2
    half = n // 2
    ends = [ref[pl.ds(1, n, stride=2)] for ref in (own, other)]
    largest = jnp.max(jnp.maximum(ends[0], ends[1]), axis=0, keepdims=True)
    factor = STEP / (jnp.max(largest, axis=1, keepdims=True) + EPS)
    core = lax.axis_index("core")
    for held, base in ((own, core * half), (other, half - core * half)):
        for r in range(0, half, CHUNK):
            to = pl.ds(pl.multiple_of(base + r, CHUNK), CHUNK)
            first = held[pl.ds(2 * r, CHUNK, stride=2)]
            second = held[pl.ds(2 * (half + r), CHUNK, stride=2)]
            for p, moved in enumerate(interleave(first, second)):
                out[p, to] = jnp.clip(porosity[p, to] - factor * moved, 0.0, 1.0)


def shards(adjoint, fwd_velocity, reynolds, weights, porosity, flags):
    planes, rows, depth = porosity.shape
    points = lax.axis_size("zhi")
    cores = lax.axis_size("core")
    spaces = lax.axis_size("zlo") * lax.axis_size("x") * lax.axis_size("y")

    def pairs(start):
        there = [(i, i + 1) for i in range(start, spaces - 1, 2)]
        return there + [(j, i) for i, j in there]

    def swap(value, start):
        return lax.ppermute(value, SPACE, pairs(start))

    half_state = shape(4, planes, rows, depth)
    field = shape(planes, rows, depth)
    plane = shape(4, rows, depth)
    pair = shape(2, rows, depth)
    first, second, far = call(
        take_planes,
        [VM],
        [pair, pair, plane],
    )(adjoint)
    halo_first = swap(first, 1)
    halo_far = swap(far, 0)
    halo_second = swap(second, 1)
    part, factor, scaled = call(first_local, [SM] + [VM] * 6, [half_state, field, field], flops=1000000)(
        reynolds, first, second, far, fwd_velocity, porosity, flags
    )
    (first,) = call(near_first, [VM] * 4, [pair], flops=4000000000)(part, factor, scaled, halo_first)
    halo_first = swap(first, 1)
    (far,) = call(far_all, [VM] * 5, [plane], flops=4000000000)(part, factor, scaled, halo_far, first)
    halo_far = swap(far, 0)
    (second,) = call(near_second, [VM] * 4, [pair], flops=4000000000)(part, factor, halo_second, far)
    halo_second = swap(second, 1)
    part, pull = call(
        second_local,
        [SM, SM] + [VM] * 7,
        [half_state, shape(3, planes, rows, depth)],
        flops=4000000000,
    )(reynolds, weights, first, second, far, fwd_velocity, porosity, flags, scaled)
    half = shape(planes, rows // cores, depth)
    held, mine, theirs = call(
        second_join,
        [VM] * 7,
        [shape(planes, 4, rows, depth), half, half],
        scratch=[pltpu.VMEM((planes, rows, depth), F32)] * 2,
    )(part, factor, scaled, pull, halo_first, halo_second, halo_far)
    other = lax.ppermute(theirs, "core", [(0, 1), (1, 0)])
    (state,) = call(
        write_state,
        [VM],
        [shape(1, 4, planes, rows, depth)],
        specs=[HB],
        scratch=[pltpu.SemaphoreType.DMA((2,))],
    )(held)
    group = points * spaces
    (blocks,) = call(add_cores, [VM, VM], [shape(group, depth)])(mine, other)
    blocks = lax.all_to_all(blocks.reshape(group, 1, depth), SPACE + ("zhi",), 0, 0, tiled=True)
    (copies,) = call(functools.partial(filter_planes, points), [VM], [shape(2 * group, depth)])(
        blocks.reshape(group, depth)
    )
    own = lax.all_to_all(copies.reshape(group, 2, depth), SPACE + ("zhi",), 0, 0, tiled=True)
    own = own.reshape(2 * group, depth)
    other = lax.ppermute(own, "core", [(0, 1), (1, 0)])
    (porosity_new,) = call(update, [VM] * 3, [field])(porosity, own, other)
    return state, porosity_new


def solution(mesh):
    fine = Mesh(mesh.devices.reshape(4, 2, 4, 4, 4), POINT + SPACE)
    return jax.shard_map(
        shards,
        mesh=fine,
        in_specs=(
            P(POINT, None, SPACE, None, None),
            P(POINT, None, SPACE, None, None),
            P(POINT),
            P(),
            P(SPACE, None, None),
            P(SPACE, None, None),
        ),
        out_specs=(P(POINT, None, SPACE, None, None), P(SPACE, None, None)),
        check_vma=False,
    )
```

```python
import functools

import jax
import jax.numpy as jnp
from jax import lax
from jax.experimental import pallas as pl
from jax.experimental.pallas import tpu as pltpu
from jax.sharding import Mesh
from jax.sharding import PartitionSpec as P

AMAX = 50.0
QRAMP = 0.1
BETA = 0.5
STEP = 0.2
EPS = 1e-06

POINT = ("zhi", "core")
SPACE = ("zlo", "x", "y")
CHUNK = 32
VM = pl.BlockSpec(memory_space=pltpu.VMEM)
SM = pl.BlockSpec(memory_space=pltpu.SMEM)
HB = pl.BlockSpec(memory_space=pltpu.HBM)
F32 = jnp.float32


def shape(*dims):
    return jax.ShapeDtypeStruct(dims, F32)


def call(body, ins, outs, specs=None, scratch=(), vmem=32.0, flops=1_000_000):
    return pl.pallas_call(
        body,
        in_specs=ins,
        out_specs=[VM] * len(outs) if specs is None else specs,
        out_shape=list(outs),
        scratch_shapes=list(scratch),
        compiler_params=pltpu.CompilerParams(vmem_limit_bytes=int(vmem * 2**20)),
        cost_estimate=pl.CostEstimate(flops=flops, bytes_accessed=4_000_000, transcendentals=0),
    )


def row_shift(read, r, size, rows):
    at = lax.broadcasted_iota(jnp.int32, (size, 128), 0)
    if r == 0:
        before = jnp.where(at == 0, 0.0, pltpu.roll(read(0, size), 1, 0))
    else:
        before = read(r - 1, size)
    if r + size == rows:
        after = jnp.where(at == size - 1, 0.0, pltpu.roll(read(r, size), size - 1, 0))
    else:
        after = read(r + 1, size)
    return before, after


def lane_shift(value):
    at = lax.broadcasted_iota(jnp.int32, value.shape, 1)
    last = value.shape[1] - 1
    before = jnp.where(at == 0, 0.0, pltpu.roll(value, 1, 1))
    after = jnp.where(at == last, 0.0, pltpu.roll(value, last, 1))
    return before, after


def side(p):
    place = lax.axis_index("zlo") * lax.axis_size("x") + lax.axis_index("x")
    odd = lax.rem(place * lax.axis_size("y") + lax.axis_index("y"), 2)
    index = odd if p == 0 else 1 - odd
    return index, (1 - 2 * index).astype(F32)


def reader(first, second, far):
    def read(c, p, r, n):
        if p == 1:
            return far[c, r : r + n]
        if c in (1, 2):
            return second[c - 1, r : r + n]
        return first[min(c, 1), r : r + n]

    return read


def local_chunk(read, p, sign, r, size, rows, u, nu, scale, drive):
    ux, uy, uz = [0.5 * v for v in u]
    inner = nu + sign * ux
    outer = nu - sign * ux
    y_after, y_before = nu + uy, nu - uy
    z_after, z_before = nu + uz, nu - uz
    mu = read(3, p, r, size)
    mu_in = read(3, 1 - p, r, size)
    mu_ym, mu_yp = row_shift(lambda a, n: read(3, p, a, n), r, size, rows)
    mu_zm, mu_zp = lane_shift(mu)
    gradient = [(0.5 * sign) * mu_in, 0.5 * (mu_yp - mu_ym), 0.5 * (mu_zp - mu_zm)]
    parts = []
    diverge = None
    for c in range(3):
        lam = read(c, p, r, size)
        lam_in = read(c, 1 - p, r, size)
        ym, yp = row_shift(lambda a, n: read(c, p, a, n), r, size, rows)
        zm, zp = lane_shift(lam)
        total = lam + inner * lam_in + y_after * yp + y_before * ym + z_after * zp + z_before * zm
        total = total - gradient[c] + u[c] * drive
        parts.append(scale * total)
        term = (sign * lam_in, yp - ym, zp - zm)[c]
        diverge = term if diverge is None else diverge + term
    parts.append(mu - (0.5 * BETA) * diverge)
    return parts, scale * outer


def viscosity_of(reynolds):
    return 20.0 / jnp.full((1, 128), reynolds[0], F32)


def first_local(reynolds, first, second, far, vel, porosity, flags, part, factor, scaled):
    rows = far.shape[1]
    nu = viscosity_of(reynolds)
    read = reader(first, second, far)
    for p in range(2):
        index, sign = side(p)
        for r in range(0, rows, CHUNK):
            now = slice(r, r + CHUNK)
            por = porosity[index, now]
            flag = flags[index, now]
            alpha = (AMAX * QRAMP) * (1.0 - por) / (QRAMP + por)
            scale = jnp.where(flag != 1, 1.0, 0.0) / (1.0 + 6.0 * nu + alpha)
            drive = jnp.where(flag == 2, 1.0, 0.0) - alpha
            u = [vel[0, d, index, now].astype(F32) for d in range(3)]
            parts, outer = local_chunk(read, p, sign, r, CHUNK, rows, u, nu, scale, drive)
            for c in range(4):
                part[c, p, now] = parts[c]
            factor[p, now] = outer
            scaled[p, now] = scale


def join_first(part, factor, scaled, halo, p, sign, now):
    lam, mu = halo
    outer = part[0, p, now] + factor[p, now] * lam + (0.5 * sign) * (scaled[p, now] * mu)
    return outer, part[3, p, now] + (0.5 * BETA * sign) * lam


def join_second(part, factor, halo, p, now):
    outer = factor[p, now]
    return [part[c + 1, p, now] + outer * halo[c] for c in range(2)]


def near_first(part, factor, scaled, halo, out):
    _, sign = side(0)
    for r in range(0, halo.shape[1], CHUNK):
        now = slice(r, r + CHUNK)
        out[0, now], out[1, now] = join_first(
            part, factor, scaled, (halo[0, now], halo[1, now]), 0, sign, now
        )


def near_second(part, factor, halo, after, out):
    for r in range(0, halo.shape[1], CHUNK):
        now = slice(r, r + CHUNK)
        out[0, now], out[1, now] = join_second(part, factor, (halo[0, now], halo[1, now]), 0, now)


def far_all(part, factor, scaled, halo, after, out):
    _, sign = side(1)
    for r in range(0, halo.shape[1], CHUNK):
        now = slice(r, r + CHUNK)
        out[0, now], out[3, now] = join_first(
            part, factor, scaled, (halo[0, now], halo[3, now]), 1, sign, now
        )
        out[1, now], out[2, now] = join_second(part, factor, (halo[1, now], halo[2, now]), 1, now)


def second_local(
    reynolds, weights, first, second, far, vel, porosity, flags, scaled, part, pull
):
    rows = far.shape[1]
    point = lax.axis_index("zhi") * lax.axis_size("core") + lax.axis_index("core")
    nu = viscosity_of(reynolds)
    whole = weights[0]
    for i in range(1, weights.shape[0]):
        whole = whole + weights[i]
    share = jnp.full((1, 128), weights[point].astype(F32), F32) / jnp.full(
        (1, 128), whole.astype(F32), F32
    )
    read = reader(first, second, far)
    for p in range(2):
        index, sign = side(p)
        for r in range(0, rows, CHUNK):
            now = slice(r, r + CHUNK)
            por = porosity[index, now]
            inverse = 1.0 / (QRAMP + por)
            alpha = (AMAX * QRAMP) * (1.0 - por) * inverse
            drive = jnp.where(flags[index, now] == 2, 1.0, 0.0) - alpha
            u = [vel[0, d, index, now].astype(F32) for d in range(3)]
            parts, _ = local_chunk(read, p, sign, r, CHUNK, rows, u, nu, scaled[p, now], drive)
            slope = (-AMAX * QRAMP * (1.0 + QRAMP)) * (inverse * inverse) * share
            for c in range(4):
                part[c, p, now] = parts[c]
            for c in range(3):
                pull[c, p, now] = slope * u[c]


def counts(at, whole):
    return 4.0 - jnp.where(at == 0, 1.0, 0.0) - jnp.where(at == whole - 1, 1.0, 0.0)


def second_join(
    part, factor, scaled, pull, first, second, far, held, mine, theirs, sens, weighted
):
    rows = far.shape[1]
    read = reader(first, second, far)
    for p in range(2):
        _, sign = side(p)
        for r in range(0, rows, CHUNK):
            now = slice(r, r + CHUNK)
            halo = [read(c, p, r, CHUNK) for c in range(4)]
            lam0, mu = join_first(part, factor, scaled, (halo[0], halo[3]), p, sign, now)
            lam1, lam2 = join_second(part, factor, halo[1:3], p, now)
            held[p, 0, now] = lam0
            held[p, 1, now] = lam1
            held[p, 2, now] = lam2
            held[p, 3, now] = mu
            sens[p, now] = pull[0, p, now] * lam0 + pull[1, p, now] * lam1 + pull[2, p, now] * lam2
    half = rows // 2
    core = lax.axis_index("core")
    lane = lax.broadcasted_iota(jnp.int32, (1, 128), 1)
    row = lax.broadcasted_iota(jnp.int32, (CHUNK, 128), 0)
    along_z = 1.0 / counts(lane, 128)
    inner = along_z * 0.25
    for p in range(2):
        index, _ = side(p)
        for r in range(0, rows, CHUNK):
            read = lambda a, n: sens[p, a : a + n]
            ym, yp = row_shift(read, r, CHUNK, rows)
            along = ym + yp + 2.0 * read(r, CHUNK)
            zm, zp = lane_shift(along)
            if r == 0 or r + CHUNK == rows:
                scale = along_z / counts(row + r, rows)
            else:
                scale = inner
            weighted[index, r : r + CHUNK] = (zm + zp + 2.0 * along) * scale
    for owner, (kept, sent) in enumerate(((0, half), (half, 0))):

        @pl.when(core == owner)
        def _():
            for p in range(2):
                mine[p] = weighted[p, kept : kept + half]
                theirs[p] = weighted[p, sent : sent + half]


def write_state(held, state, sems):
    copies = [
        pltpu.make_async_copy(held.at[p], state.at[0, :, side(p)[0]], sems.at[p]) for p in range(2)
    ]
    for copy in copies:
        copy.start()
    for copy in copies:
        copy.wait()


def left_half(shape):
    return lax.broadcasted_iota(jnp.int32, shape, 1) < shape[1] // 2


def swap_halves(value):
    return pltpu.roll(value, value.shape[1] // 2, 1)


def interleave(one, two):
    left = left_half(one.shape)
    return jnp.where(left, one, swap_halves(two)), jnp.where(left, swap_halves(one), two)


def add_cores(mine, other, blocks):
    half = mine.shape[1]
    for r in range(0, half, CHUNK):
        now = slice(r, r + CHUNK)
        first, second = interleave(mine[0, now] + other[0, now], mine[1, now] + other[1, now])
        blocks[now] = first
        blocks[half + r : half + r + CHUNK] = second


def filter_planes(points, blocks, out):
    slabs = blocks.shape[0] // points
    total = blocks[pl.ds(0, slabs, stride=points)]
    for q in range(1, points):
        total = total + blocks[pl.ds(q, slabs, stride=points)]
    swapped = swap_halves(total)
    at = lax.broadcasted_iota(jnp.int32, total.shape, 0)
    left = left_half(total.shape)
    below = jnp.where(at == 0, 0.0, pltpu.roll(swapped, 1, 0))
    above = jnp.where(at == slabs - 1, 0.0, pltpu.roll(swapped, slabs - 1, 0))
    plane = 2 * at + jnp.where(left, 0, 1)
    filtered = (2.0 * total + swapped + jnp.where(left, below, above)) / counts(plane, 2 * slabs)
    largest = jnp.broadcast_to(jnp.max(jnp.abs(filtered), axis=0, keepdims=True), total.shape)
    for q in range(points):
        out[pl.ds(2 * q, slabs, stride=2 * points)] = filtered
        out[pl.ds(2 * q + 1, slabs, stride=2 * points)] = largest


def update(porosity, own, other, out):
    n = own.shape[0] // 2
    half = n // 2
    ends = [ref[pl.ds(1, n, stride=2)] for ref in (own, other)]
    largest = jnp.max(jnp.maximum(ends[0], ends[1]), axis=0, keepdims=True)
    factor = STEP / (jnp.max(largest, axis=1, keepdims=True) + EPS)
    core = lax.axis_index("core")
    for held, base in ((own, core * half), (other, half - core * half)):
        for r in range(0, half, CHUNK):
            to = pl.ds(pl.multiple_of(base + r, CHUNK), CHUNK)
            first = held[pl.ds(2 * r, CHUNK, stride=2)]
            second = held[pl.ds(2 * (half + r), CHUNK, stride=2)]
            for p, moved in enumerate(interleave(first, second)):
                out[p, to] = jnp.clip(porosity[p, to] - factor * moved, 0.0, 1.0)


def shards(adjoint, fwd_velocity, reynolds, weights, porosity, flags):
    planes, rows, depth = porosity.shape
    points = lax.axis_size("zhi")
    cores = lax.axis_size("core")
    spaces = lax.axis_size("zlo") * lax.axis_size("x") * lax.axis_size("y")

    def pairs(start):
        there = [(i, i + 1) for i in range(start, spaces - 1, 2)]
        return there + [(j, i) for i, j in there]

    def swap(value, start):
        return lax.ppermute(value, SPACE, pairs(start))

    half_state = shape(4, planes, rows, depth)
    field = shape(planes, rows, depth)
    plane = shape(4, rows, depth)
    pair = shape(2, rows, depth)
    place = (lax.axis_index("zlo") * lax.axis_size("x") + lax.axis_index("x")) * lax.axis_size("y")
    odd = lax.rem(place + lax.axis_index("y"), 2)
    near = lax.dynamic_index_in_dim(adjoint[0], odd, 1, keepdims=False)
    first, second = near[0::3], near[1:3]
    far = lax.dynamic_index_in_dim(adjoint[0], 1 - odd, 1, keepdims=False)
    halo_first = swap(first, 1)
    halo_far = swap(far, 0)
    halo_second = swap(second, 1)
    part, factor, scaled = call(first_local, [SM] + [VM] * 6, [half_state, field, field], flops=1000000)(
        reynolds, first, second, far, fwd_velocity, porosity, flags
    )
    (first,) = call(near_first, [VM] * 4, [pair], flops=4000000000)(part, factor, scaled, halo_first)
    halo_first = swap(first, 1)
    (far,) = call(far_all, [VM] * 5, [plane], flops=4000000000)(part, factor, scaled, halo_far, first)
    halo_far = swap(far, 0)
    (second,) = call(near_second, [VM] * 4, [pair], flops=4000000000)(part, factor, halo_second, far)
    halo_second = swap(second, 1)
    part, pull = call(
        second_local,
        [SM, SM] + [VM] * 7,
        [half_state, shape(3, planes, rows, depth)],
        flops=4000000000,
    )(reynolds, weights, first, second, far, fwd_velocity, porosity, flags, scaled)
    half = shape(planes, rows // cores, depth)
    held, mine, theirs = call(
        second_join,
        [VM] * 7,
        [shape(planes, 4, rows, depth), half, half],
        scratch=[pltpu.VMEM((planes, rows, depth), F32)] * 2,
    )(part, factor, scaled, pull, halo_first, halo_second, halo_far)
    other = lax.ppermute(theirs, "core", [(0, 1), (1, 0)])
    (state,) = call(
        write_state,
        [VM],
        [shape(1, 4, planes, rows, depth)],
        specs=[HB],
        scratch=[pltpu.SemaphoreType.DMA((2,))],
    )(held)
    group = points * spaces
    (blocks,) = call(add_cores, [VM, VM], [shape(group, depth)])(mine, other)
    blocks = lax.all_to_all(blocks.reshape(group, 1, depth), SPACE + ("zhi",), 0, 0, tiled=True)
    (copies,) = call(functools.partial(filter_planes, points), [VM], [shape(2 * group, depth)])(
        blocks.reshape(group, depth)
    )
    own = lax.all_to_all(copies.reshape(group, 2, depth), SPACE + ("zhi",), 0, 0, tiled=True)
    own = own.reshape(2 * group, depth)
    other = lax.ppermute(own, "core", [(0, 1), (1, 0)])
    (porosity_new,) = call(update, [VM] * 3, [field])(porosity, own, other)
    return state, porosity_new


def solution(mesh):
    fine = Mesh(mesh.devices.reshape(4, 2, 4, 4, 4), POINT + SPACE)
    return jax.shard_map(
        shards,
        mesh=fine,
        in_specs=(
            P(POINT, None, SPACE, None, None),
            P(POINT, None, SPACE, None, None),
            P(POINT),
            P(),
            P(SPACE, None, None),
            P(SPACE, None, None),
        ),
        out_specs=(P(POINT, None, SPACE, None, None), P(SPACE, None, None)),
        check_vma=False,
    )
```

```python
import functools

import jax
import jax.numpy as jnp
from jax import lax
from jax.experimental import pallas as pl
from jax.experimental.pallas import tpu as pltpu
from jax.sharding import Mesh
from jax.sharding import PartitionSpec as P

AMAX = 50.0
QRAMP = 0.1
BETA = 0.5
STEP = 0.2
EPS = 1e-06

POINT = ("zhi", "core")
SPACE = ("zlo", "x", "y")
CHUNK = 32
VM = pl.BlockSpec(memory_space=pltpu.VMEM)
SM = pl.BlockSpec(memory_space=pltpu.SMEM)
HB = pl.BlockSpec(memory_space=pltpu.HBM)
F32 = jnp.float32


def shape(*dims):
    return jax.ShapeDtypeStruct(dims, F32)


def call(body, ins, outs, specs=None, scratch=(), vmem=32.0, flops=1_000_000):
    return pl.pallas_call(
        body,
        in_specs=ins,
        out_specs=[VM] * len(outs) if specs is None else specs,
        out_shape=list(outs),
        scratch_shapes=list(scratch),
        compiler_params=pltpu.CompilerParams(vmem_limit_bytes=int(vmem * 2**20)),
        cost_estimate=pl.CostEstimate(flops=flops, bytes_accessed=4_000_000, transcendentals=0),
    )


def row_shift(read, r, size, rows):
    at = lax.broadcasted_iota(jnp.int32, (size, 128), 0)
    if r == 0:
        before = jnp.where(at == 0, 0.0, pltpu.roll(read(0, size), 1, 0))
    else:
        before = read(r - 1, size)
    if r + size == rows:
        after = jnp.where(at == size - 1, 0.0, pltpu.roll(read(r, size), size - 1, 0))
    else:
        after = read(r + 1, size)
    return before, after


def lane_shift(value):
    at = lax.broadcasted_iota(jnp.int32, value.shape, 1)
    last = value.shape[1] - 1
    before = jnp.where(at == 0, 0.0, pltpu.roll(value, 1, 1))
    after = jnp.where(at == last, 0.0, pltpu.roll(value, last, 1))
    return before, after


def side(p):
    place = lax.axis_index("zlo") * lax.axis_size("x") + lax.axis_index("x")
    odd = lax.rem(place * lax.axis_size("y") + lax.axis_index("y"), 2)
    index = odd if p == 0 else 1 - odd
    return index, (1 - 2 * index).astype(F32)


def reader(first, second, far):
    def read(c, p, r, n):
        if p == 1:
            return far[c, r : r + n]
        if c in (1, 2):
            return second[c - 1, r : r + n]
        return first[min(c, 1), r : r + n]

    return read


def take_planes(adjoint, first, second, far):
    index, _ = side(0)
    for r in range(0, far.shape[1], CHUNK):
        now = slice(r, r + CHUNK)
        first[0, now] = adjoint[0, 0, index, now]
        first[1, now] = adjoint[0, 3, index, now]
        for c in range(2):
            second[c, now] = adjoint[0, c + 1, index, now]
        for c in range(4):
            far[c, now] = adjoint[0, c, 1 - index, now]


def local_chunk(read, p, sign, r, size, rows, u, nu, scale, drive):
    ux, uy, uz = [0.5 * v for v in u]
    inner = nu + sign * ux
    outer = nu - sign * ux
    y_after, y_before = nu + uy, nu - uy
    z_after, z_before = nu + uz, nu - uz
    mu = read(3, p, r, size)
    mu_in = read(3, 1 - p, r, size)
    mu_ym, mu_yp = row_shift(lambda a, n: read(3, p, a, n), r, size, rows)
    mu_zm, mu_zp = lane_shift(mu)
    gradient = [(0.5 * sign) * mu_in, 0.5 * (mu_yp - mu_ym), 0.5 * (mu_zp - mu_zm)]
    parts = []
    diverge = None
    for c in range(3):
        lam = read(c, p, r, size)
        lam_in = read(c, 1 - p, r, size)
        ym, yp = row_shift(lambda a, n: read(c, p, a, n), r, size, rows)
        zm, zp = lane_shift(lam)
        total = lam + inner * lam_in + y_after * yp + y_before * ym + z_after * zp + z_before * zm
        total = total - gradient[c] + u[c] * drive
        parts.append(scale * total)
        term = (sign * lam_in, yp - ym, zp - zm)[c]
        diverge = term if diverge is None else diverge + term
    parts.append(mu - (0.5 * BETA) * diverge)
    return parts, scale * outer


def viscosity_of(reynolds):
    return 20.0 / jnp.full((1, 128), reynolds[0], F32)


def first_local(reynolds, first, second, far, vel, porosity, flags, part, factor, scaled):
    rows = far.shape[1]
    nu = viscosity_of(reynolds)
    read = reader(first, second, far)
    for p in range(2):
        index, sign = side(p)
        for r in range(0, rows, CHUNK):
            now = slice(r, r + CHUNK)
            por = porosity[index, now]
            flag = flags[index, now]
            alpha = (AMAX * QRAMP) * (1.0 - por) / (QRAMP + por)
            scale = jnp.where(flag != 1, 1.0, 0.0) / (1.0 + 6.0 * nu + alpha)
            drive = jnp.where(flag == 2, 1.0, 0.0) - alpha
            u = [vel[0, d, index, now].astype(F32) for d in range(3)]
            parts, outer = local_chunk(read, p, sign, r, CHUNK, rows, u, nu, scale, drive)
            for c in range(4):
                part[c, p, now] = parts[c]
            factor[p, now] = outer
            scaled[p, now] = scale


def join_first(part, factor, scaled, halo, p, sign, now):
    lam, mu = halo
    outer = part[0, p, now] + factor[p, now] * lam + (0.5 * sign) * (scaled[p, now] * mu)
    return outer, part[3, p, now] + (0.5 * BETA * sign) * lam


def join_second(part, factor, halo, p, now):
    outer = factor[p, now]
    return [part[c + 1, p, now] + outer * halo[c] for c in range(2)]


def near_first(part, factor, scaled, halo, out):
    _, sign = side(0)
    for r in range(0, halo.shape[1], CHUNK):
        now = slice(r, r + CHUNK)
        out[0, now], out[1, now] = join_first(
            part, factor, scaled, (halo[0, now], halo[1, now]), 0, sign, now
        )


def near_second(part, factor, halo, after, out):
    for r in range(0, halo.shape[1], CHUNK):
        now = slice(r, r + CHUNK)
        out[0, now], out[1, now] = join_second(part, factor, (halo[0, now], halo[1, now]), 0, now)


def far_all(part, factor, scaled, halo, after, out):
    _, sign = side(1)
    for r in range(0, halo.shape[1], CHUNK):
        now = slice(r, r + CHUNK)
        out[0, now], out[3, now] = join_first(
            part, factor, scaled, (halo[0, now], halo[3, now]), 1, sign, now
        )
        out[1, now], out[2, now] = join_second(part, factor, (halo[1, now], halo[2, now]), 1, now)


def second_local(
    reynolds, weights, first, second, far, vel, porosity, flags, scaled, part, pull
):
    rows = far.shape[1]
    point = lax.axis_index("zhi") * lax.axis_size("core") + lax.axis_index("core")
    nu = viscosity_of(reynolds)
    whole = weights[0]
    for i in range(1, weights.shape[0]):
        whole = whole + weights[i]
    share = jnp.full((1, 128), weights[point].astype(F32), F32) / jnp.full(
        (1, 128), whole.astype(F32), F32
    )
    read = reader(first, second, far)
    for p in range(2):
        index, sign = side(p)
        for r in range(0, rows, CHUNK):
            now = slice(r, r + CHUNK)
            por = porosity[index, now]
            inverse = 1.0 / (QRAMP + por)
            alpha = (AMAX * QRAMP) * (1.0 - por) * inverse
            drive = jnp.where(flags[index, now] == 2, 1.0, 0.0) - alpha
            u = [vel[0, d, index, now].astype(F32) for d in range(3)]
            parts, _ = local_chunk(read, p, sign, r, CHUNK, rows, u, nu, scaled[p, now], drive)
            slope = (-AMAX * QRAMP * (1.0 + QRAMP)) * (inverse * inverse) * share
            for c in range(4):
                part[c, p, now] = parts[c]
            for c in range(3):
                pull[c, p, now] = slope * u[c]


def counts(at, whole):
    return 4.0 - jnp.where(at == 0, 1.0, 0.0) - jnp.where(at == whole - 1, 1.0, 0.0)


def second_join(
    part, factor, scaled, pull, first, second, far, held, mine, theirs, sens, weighted
):
    rows = far.shape[1]
    read = reader(first, second, far)
    for p in range(2):
        _, sign = side(p)
        for r in range(0, rows, CHUNK):
            now = slice(r, r + CHUNK)
            halo = [read(c, p, r, CHUNK) for c in range(4)]
            lam0, mu = join_first(part, factor, scaled, (halo[0], halo[3]), p, sign, now)
            lam1, lam2 = join_second(part, factor, halo[1:3], p, now)
            held[p, 0, now] = lam0
            held[p, 1, now] = lam1
            held[p, 2, now] = lam2
            held[p, 3, now] = mu
            sens[p, now] = pull[0, p, now] * lam0 + pull[1, p, now] * lam1 + pull[2, p, now] * lam2
    half = rows // 2
    core = lax.axis_index("core")
    lane = lax.broadcasted_iota(jnp.int32, (1, 128), 1)
    row = lax.broadcasted_iota(jnp.int32, (CHUNK, 128), 0)
    along_z = 1.0 / counts(lane, 128)
    inner = along_z * 0.25
    for p in range(2):
        index, _ = side(p)
        for r in range(0, rows, CHUNK):
            read = lambda a, n: sens[p, a : a + n]
            ym, yp = row_shift(read, r, CHUNK, rows)
            along = ym + yp + 2.0 * read(r, CHUNK)
            zm, zp = lane_shift(along)
            if r == 0 or r + CHUNK == rows:
                scale = along_z / counts(row + r, rows)
            else:
                scale = inner
            weighted[index, r : r + CHUNK] = (zm + zp + 2.0 * along) * scale
    for owner, (kept, sent) in enumerate(((0, half), (half, 0))):

        @pl.when(core == owner)
        def _():
            for out, base in ((mine, kept), (theirs, sent)):
                for r in range(0, half, CHUNK):
                    now = slice(base + r, base + r + CHUNK)
                    out[r : r + CHUNK], out[half + r : half + r + CHUNK] = interleave(
                        weighted[0, now], weighted[1, now]
                    )


def write_state(held, state, sems):
    copies = [
        pltpu.make_async_copy(held.at[p], state.at[0, :, side(p)[0]], sems.at[p]) for p in range(2)
    ]
    for copy in copies:
        copy.start()
    for copy in copies:
        copy.wait()


def left_half(shape):
    return lax.broadcasted_iota(jnp.int32, shape, 1) < shape[1] // 2


def swap_halves(value):
    return pltpu.roll(value, value.shape[1] // 2, 1)


def interleave(one, two):
    left = left_half(one.shape)
    return jnp.where(left, one, swap_halves(two)), jnp.where(left, swap_halves(one), two)


def add_cores(mine, other, blocks):
    for r in range(0, blocks.shape[0], CHUNK):
        now = slice(r, r + CHUNK)
        blocks[now] = mine[now] + other[now]


def filter_planes(points, blocks, out):
    slabs = blocks.shape[0] // points
    total = blocks[pl.ds(0, slabs, stride=points)]
    for q in range(1, points):
        total = total + blocks[pl.ds(q, slabs, stride=points)]
    swapped = swap_halves(total)
    at = lax.broadcasted_iota(jnp.int32, total.shape, 0)
    left = left_half(total.shape)
    below = jnp.where(at == 0, 0.0, pltpu.roll(swapped, 1, 0))
    above = jnp.where(at == slabs - 1, 0.0, pltpu.roll(swapped, slabs - 1, 0))
    plane = 2 * at + jnp.where(left, 0, 1)
    filtered = (2.0 * total + swapped + jnp.where(left, below, above)) / counts(plane, 2 * slabs)
    largest = jnp.broadcast_to(jnp.max(jnp.abs(filtered), axis=0, keepdims=True), total.shape)
    for q in range(points):
        out[pl.ds(2 * q, slabs, stride=2 * points)] = filtered
        out[pl.ds(2 * q + 1, slabs, stride=2 * points)] = largest


def update(porosity, own, other, out):
    n = own.shape[0] // 2
    half = n // 2
    ends = [ref[pl.ds(1, n, stride=2)] for ref in (own, other)]
    largest = jnp.max(jnp.maximum(ends[0], ends[1]), axis=0, keepdims=True)
    factor = STEP / (jnp.max(largest, axis=1, keepdims=True) + EPS)
    core = lax.axis_index("core")
    for held, base in ((own, core * half), (other, half - core * half)):
        for r in range(0, half, CHUNK):
            to = pl.ds(pl.multiple_of(base + r, CHUNK), CHUNK)
            first = held[pl.ds(2 * r, CHUNK, stride=2)]
            second = held[pl.ds(2 * (half + r), CHUNK, stride=2)]
            for p, moved in enumerate(interleave(first, second)):
                out[p, to] = jnp.clip(porosity[p, to] - factor * moved, 0.0, 1.0)


def shards(adjoint, fwd_velocity, reynolds, weights, porosity, flags):
    planes, rows, depth = porosity.shape
    points = lax.axis_size("zhi")
    cores = lax.axis_size("core")
    spaces = lax.axis_size("zlo") * lax.axis_size("x") * lax.axis_size("y")

    def pairs(start):
        there = [(i, i + 1) for i in range(start, spaces - 1, 2)]
        return there + [(j, i) for i, j in there]

    def swap(value, start):
        return lax.ppermute(value, SPACE, pairs(start))

    half_state = shape(4, planes, rows, depth)
    field = shape(planes, rows, depth)
    plane = shape(4, rows, depth)
    pair = shape(2, rows, depth)
    first, second, far = call(
        take_planes,
        [VM],
        [pair, pair, plane],
    )(adjoint)
    halo_first = swap(first, 1)
    halo_far = swap(far, 0)
    halo_second = swap(second, 1)
    part, factor, scaled = call(first_local, [SM] + [VM] * 6, [half_state, field, field], flops=1000000)(
        reynolds, first, second, far, fwd_velocity, porosity, flags
    )
    (first,) = call(near_first, [VM] * 4, [pair], flops=4000000000)(part, factor, scaled, halo_first)
    halo_first = swap(first, 1)
    (far,) = call(far_all, [VM] * 5, [plane], flops=4000000000)(part, factor, scaled, halo_far, first)
    halo_far = swap(far, 0)
    (second,) = call(near_second, [VM] * 4, [pair], flops=4000000000)(part, factor, halo_second, far)
    halo_second = swap(second, 1)
    part, pull = call(
        second_local,
        [SM, SM] + [VM] * 7,
        [half_state, shape(3, planes, rows, depth)],
        flops=4000000000,
    )(reynolds, weights, first, second, far, fwd_velocity, porosity, flags, scaled)
    half = shape(planes * rows // cores, depth)
    held, mine, theirs = call(
        second_join,
        [VM] * 7,
        [shape(planes, 4, rows, depth), half, half],
        scratch=[pltpu.VMEM((planes, rows, depth), F32)] * 2,
    )(part, factor, scaled, pull, halo_first, halo_second, halo_far)
    other = lax.ppermute(theirs, "core", [(0, 1), (1, 0)])
    (state,) = call(
        write_state,
        [VM],
        [shape(1, 4, planes, rows, depth)],
        specs=[HB],
        scratch=[pltpu.SemaphoreType.DMA((2,))],
    )(held)
    group = points * spaces
    (blocks,) = call(add_cores, [VM, VM], [shape(group, depth)])(mine, other)
    blocks = lax.all_to_all(blocks.reshape(group, 1, depth), SPACE + ("zhi",), 0, 0, tiled=True)
    (copies,) = call(functools.partial(filter_planes, points), [VM], [shape(2 * group, depth)])(
        blocks.reshape(group, depth)
    )
    own = lax.all_to_all(copies.reshape(group, 2, depth), SPACE + ("zhi",), 0, 0, tiled=True)
    own = own.reshape(2 * group, depth)
    other = lax.ppermute(own, "core", [(0, 1), (1, 0)])
    (porosity_new,) = call(update, [VM] * 3, [field])(porosity, own, other)
    return state, porosity_new


def solution(mesh):
    fine = Mesh(mesh.devices.reshape(4, 2, 4, 4, 4), POINT + SPACE)
    return jax.shard_map(
        shards,
        mesh=fine,
        in_specs=(
            P(POINT, None, SPACE, None, None),
            P(POINT, None, SPACE, None, None),
            P(POINT),
            P(),
            P(SPACE, None, None),
            P(SPACE, None, None),
        ),
        out_specs=(P(POINT, None, SPACE, None, None), P(SPACE, None, None)),
        check_vma=False,
    )
```
